128 devices in a mesh: tp: 32 (over y, z, x_lo), col: 4 (over x_hi, core).
Axes of the slice: x: 4 (x_hi: 2, x_lo: 2; x = x_hi * 2 + x_lo), y: 4, z: 4, core: 2. Of those that a mesh axis runs over, the one named last changes fastest.
Arguments:
- momentum: float32 [9216, 18432], P('tp', 'col'), may hold values from -2000 to 2000
Outputs:
- gram: float32 [9216, 9216], P('tp', 'col')
The draws below stay inside these ranges and needn't reach their ends.
All inputs are finite; a program needn't handle non-finite values.
Results may differ from the reference program's by a relative error of at most 0.0022.
Values may be sent and summed in bfloat16 or wider, within the bound.
A program may use at most 192 MiB of HBM per device.

```python
import jax
import jax.numpy as jnp

COLS = 18432
ROWS = 9216


def draw_momentum(key, part):
    key = jax.random.fold_in(key, 11)
    key_rows, key_cols, key_base = jax.random.split(key, 3)
    position = jnp.arange(ROWS, dtype=jnp.float32)[:, None] / ROWS
    row_scale = jnp.exp(jax.random.uniform(key_rows, (ROWS, 1), jnp.float32) * jnp.log(10.0)) * (1.0 + 2.0 * position)
    col_scale = jnp.exp(jax.random.uniform(key_cols, (1, COLS), jnp.float32) * jnp.log(10.0))
    base = jnp.clip(jax.random.normal(key_base, (ROWS, COLS), jnp.float32), -6.0, 6.0)
    return (row_scale * col_scale * base).astype(jnp.float32)


def setup_inputs(seed: int = 0) -> dict:
    key_of = jax.random.split(jax.random.key(seed), 2)
    momentum = draw_momentum(jax.random.fold_in(key_of[1], 71), 0)
    return {"momentum": momentum}


def reference(momentum):
    total = jnp.sum(momentum * momentum)
    normalized = (momentum * (1.0 / (jnp.sqrt(total) + 1e-07))).astype(jnp.bfloat16)
    product = jnp.dot(normalized, normalized.T, preferred_element_type=jnp.float32)
    return product * jnp.float32(ROWS)
```

```python
import functools

import jax
import jax.numpy as jnp
from jax import lax
from jax.experimental import pallas as pl
from jax.experimental.pallas import tpu as pltpu
from jax.sharding import PartitionSpec as P

SLOTS = ((0, 0), (1, 0), (3, 0), (0, 1), (0, 3), (2, 0), (0, 2))
OWN, Y1, Y3, Z1, Z3, Y2, Z2 = range(7)
PAIRS = (
    (OWN, OWN, False),
    (OWN, Z1, True),
    (Z3, Z1, False),
    (OWN, Y1, True),
    (Z1, Y1, True),
    (Y1, Y3, False),
    (Z1, Y3, True),
    (Z2, Y3, True),
    (Z1, Y2, True),
    (Z2, Y2, False),
)
EARLY = tuple(range(7))
LATE = tuple(range(7, 10))
QUARTER = tuple(tuple(e for e, (_, b, _) in enumerate(PAIRS) if SLOTS[b][0] == q) for q in range(4))
PARITY = tuple(tuple(sorted(QUARTER[p] + QUARTER[p + 2])) for p in range(2))
MESH = pl.DeviceIdType.MESH
F32, BF16 = jnp.float32, jnp.bfloat16
CHUNK = 384


def kernel(
    factor, m_ref, o_ref,
    slots, xsend, acc, d2, xs, xr, fb, ftb, outb, part, g8, gy, gz,
    in_sem, ps_s, ps_r, gat_s, gat_r, fwd_s, xc_s, d2_s, d2_r, x_s, x_r, f_s, f_r,
):
    rows = m_ref.shape[0]
    half = m_ref.shape[1] // 2
    cut = (half // 2) // 256 * 256
    spans = ((0, cut), (cut, half - cut))
    t, c = lax.axis_index("tp"), lax.axis_index("col")
    y, z, r = t // 8, (t // 2) % 4, t % 2
    q = (c - y + 4) % 4
    per_half = half // CHUNK

    def at(dy=0, dz=0, xl=None, dc=0):
        xl = r if xl is None else xl
        return ((((y + dy) % 4) * 4 + (z + dz) % 4) * 2 + xl, (c + dc + 4) % 4)

    core_peer = (t, c + 1 - 2 * (c % 2))
    other = 1 - r

    loads = []
    for j in range(2 * per_half):
        dst = acc.at[j // 2, pl.ds((j % 2) * rows, rows), pl.ds(0, CHUNK)]
        loads.append(pltpu.make_async_copy(m_ref.at[:, pl.ds(j * CHUNK, CHUNK)], dst, in_sem.at[j]))
        loads[-1].start()

    bar = pltpu.get_barrier_semaphore()
    me8 = r * 4 + c

    def at8(i):
        return ((y * 4 + z) * 2 + i // 4, i % 4)

    greet = [at8((me8 + o) % 8) for o in range(1, 8)]
    greet += [at(dy=o) for o in range(1, 4)] + [at(dz=o) for o in range(1, 4)]
    greet += [at(dz=1, xl=other), at(dz=3, xl=other)]
    for dy, dc in ((1, 3), (3, 1), (2, 2)):
        greet += [at(dy=dy, xl=r, dc=dc), at(dy=dy, xl=other, dc=dc)]
    for dev in greet:
        pl.semaphore_signal(bar, inc=1, device_id=dev, device_id_type=MESH)

    total = jnp.zeros((8, CHUNK), F32)
    for j in range(2 * per_half):
        loads[j].wait()
        v = acc[j // 2, (j % 2) * rows : (j % 2 + 1) * rows, 0:CHUNK]
        total += jnp.sum((v * v).reshape(rows // 8, 8, CHUNK), axis=0)
    part[0] = total[:, 0:128] + total[:, 128:256] + total[:, 256:384]
    pl.semaphore_wait(bar, len(greet))
    done = []

    def share(stage, place, me, n, device):
        place[pl.ds(me, 1)] = part[stage][None]
        copies = []
        for o in range(1, n):
            i = 8 * stage + o
            copies.append(
                pltpu.make_async_remote_copy(
                    part.at[stage], place.at[me], ps_s.at[i], ps_r.at[stage, o],
                    device_id=device(o), device_id_type=MESH,
                )
            )
            copies[-1].start()
        for o in range(1, n):
            copies[o - 1].wait_recv()
        done.extend(copies)
        return jnp.sum(place[...], axis=0)

    part[1] = share(0, g8, me8, 8, lambda o: at8((me8 + o) % 8))
    part[2] = share(1, gy, y, 4, lambda o: at(dy=o))
    whole = share(2, gz, z, 4, lambda o: at(dz=o))
    total = jnp.sum(jnp.sum(whole, axis=0, keepdims=True), axis=1, keepdims=True)
    scale = 1.0 / (jnp.sqrt(total) + 1e-07)

    def normalize(which, n0, n1, store):
        for n in range(n0, n1):
            v = acc[which * (per_half // 2) + n // 2, (n % 2) * rows : (n % 2 + 1) * rows, 0:CHUNK]
            store(n, (v * scale).astype(BF16))

    mine = pl.ds(pl.multiple_of(r * rows, 16), rows)
    theirs = pl.ds(pl.multiple_of(other * rows, 16), rows)

    def to_own(n, v):
        slots[OWN, mine, n * CHUNK : (n + 1) * CHUNK] = v

    def to_send(n, v):
        xsend[:, n * CHUNK : (n + 1) * CHUNK] = v

    def unit(slot, rr, k):
        start = pl.ds(pl.multiple_of(rr * rows, 16), rows)
        return slots.at[slot, start, pl.ds(*spans[k])]

    direct = ((Y1, at(dy=3)), (Y3, at(dy=1)), (Z1, at(dz=3)), (Z3, at(dz=1)))

    def send_own(rr, second, k):
        for i, (slot, dev) in enumerate(direct):
            cp = pltpu.make_async_remote_copy(
                unit(OWN, rr, k), unit(slot, rr, k), gat_s.at[i, second, k], gat_r.at[slot, rr, k],
                device_id=dev, device_id_type=MESH,
            )
            cp.start()
            done.append(cp)

    def arrived(slot, rr, k):
        ref = unit(slot, rr, k)
        pltpu.make_async_copy(ref, ref, gat_r.at[slot, rr, k]).wait()

    def send_x(k):
        cp = pltpu.make_async_remote_copy(
            xsend.at[:, pl.ds(*spans[k])], unit(OWN, r, k), xc_s.at[k], gat_r.at[OWN, r, k],
            device_id=at(xl=other), device_id_type=MESH,
        )
        cp.start()
        done.append(cp)

    onward = {Y1: (0, Y2, at(dy=3)), Z1: (1, Z2, at(dz=3)), Y3: (0, Y2, at(dy=1)), Z3: (1, Z2, at(dz=1))}

    def forward(slot, rr, second, k):
        i, to, dev = onward[slot]
        cp = pltpu.make_async_remote_copy(
            unit(slot, rr, k), unit(to, rr, k), fwd_s.at[i, second, k], gat_r.at[to, rr, k],
            device_id=dev, device_id_type=MESH,
        )
        cp.start()
        done.append(cp)

    first_cut = -(-cut // CHUNK)
    normalize(r, 0, first_cut, to_own)
    send_own(r, 0, 0)
    normalize(other, 0, first_cut, to_send)
    send_x(0)
    normalize(other, first_cut, per_half, to_send)
    normalize(r, first_cut, per_half, to_own)
    send_x(1)

    tile = 192

    def product(e, k):
        a, b, _ = PAIRS[e]

        def step(i, _):
            here = pl.ds(pl.multiple_of(i * tile, tile), tile)
            cols = pl.ds(*spans[k])
            p = lax.dot_general(
                slots[a, here, cols], slots[b, :, cols], (((1,), (1,)), ((), ())), preferred_element_type=F32
            )
            if k == 0:
                acc[e, here, :] = p
            else:
                acc[e, here, :] += p
            return 0

        lax.fori_loop(0, 2 * rows // tile, step, 0)

    arrived(OWN, other, 0)
    send_own(other, 1, 0)
    send_own(r, 0, 1)
    arrived(OWN, other, 1)
    send_own(other, 1, 1)
    for slot in (Y1, Z1):
        arrived(slot, r, 0)
        forward(slot, r, 0, 0)
    for slot in (Y1, Z1):
        arrived(slot, other, 0)
        forward(slot, other, 1, 0)
    for slot in (Y3, Z3):
        for rr in (r, other):
            arrived(slot, rr, 0)
    for e in EARLY:
        product(e, 0)
    for slot in (Y3, Z3):
        arrived(slot, r, 1)
        forward(slot, r, 0, 1)
    for slot in (Y3, Z3):
        arrived(slot, other, 1)
        forward(slot, other, 1, 1)
    for slot in (Y1, Z1):
        for rr in (r, other):
            arrived(slot, rr, 1)
    for e in EARLY:
        product(e, 1)

    def branches(body):
        for k in range(4):
            @pl.when(q == k)
            def _(k=k):
                body(k)

    def core_copy(k, e):
        i = PARITY[1 - k % 2].index(e)
        return pltpu.make_async_remote_copy(
            acc.at[e], d2.at[i], d2_s.at[i], d2_r.at[i], device_id=core_peer, device_id_type=MESH
        )

    def to_core(k, group):
        for e in PARITY[1 - k % 2]:
            if e in group:
                core_copy(k, e).start()

    def x_copy(e, i, kind):
        dev = (at(xl=other), at(dc=2), at(xl=other, dc=2))[kind]
        return pltpu.make_async_remote_copy(
            xs.at[i, kind], xr.at[i, kind], x_s.at[i, kind], x_r.at[i, kind], device_id=dev, device_id_type=MESH
        )

    def x_moves(k, group):
        out = []
        for e in PARITY[k % 2]:
            if e in group:
                i = QUARTER[SLOTS[PAIRS[e][1]][0]].index(e)
                if e in QUARTER[k]:
                    out.append((e, i, 0))
                else:
                    out += [(e, i, 1), (e, i, 2)]
        return out

    def to_x(k, group):
        for e in PARITY[k % 2]:
            if e in group:
                i = PARITY[k % 2].index(e)
                pltpu.make_async_copy(d2.at[i], d2.at[i], d2_r.at[i]).wait()
        for e, i, kind in x_moves(k, group):
            where = mine if kind == 1 else theirs
            j = PARITY[k % 2].index(e)
            xs[i, kind] = (acc[e, where, :] + d2[j, where, :]).astype(BF16)
            x_copy(e, i, kind).start()

    def final_copies(k, e):
        a, b, both = PAIRS[e]
        i = QUARTER[k].index(e)
        (ay, az), (by, bz) = SLOTS[a], SLOTS[b]
        copies = []
        if a != OWN:
            for n in range(2):
                copies.append(
                    pltpu.make_async_remote_copy(
                        fb.at[i, n], outb.at[(z + bz) % 4, n], f_s.at[i, n], f_r.at[(z + bz) % 4, n],
                        device_id=at(ay, az), device_id_type=MESH,
                    )
                )
        if both:
            for n in range(2):
                copies.append(
                    pltpu.make_async_remote_copy(
                        ftb.at[i, n], outb.at[(z + az) % 4, r], f_s.at[i, 2 + n], f_r.at[(z + az) % 4, r],
                        device_id=at(by, bz, xl=n, dc=ay - by), device_id_type=MESH,
                    )
                )
        return copies

    def to_final(k, group):
        for e in QUARTER[k]:
            if e not in group:
                continue
            a, b, both = PAIRS[e]
            i = QUARTER[k].index(e)
            j = PARITY[k % 2].index(e)
            for kind in range(3):
                pltpu.make_async_copy(xr.at[i, kind], xr.at[i, kind], x_r.at[i, kind]).wait()
            v = acc[e, mine, :] + d2[j, mine, :]
            for kind in range(3):
                v += xr[i, kind].astype(F32)
            v *= factor
            bz = SLOTS[b][1]
            for n in range(2):
                w = v[:, n * rows : (n + 1) * rows]
                if a == OWN:
                    outb[(z + bz) % 4, n] = w
                else:
                    fb[i, n] = w
                if both:
                    ftb[i, n] = w.T
            for cp in final_copies(k, e):
                cp.start()

    branches(lambda k: to_core(k, EARLY))
    branches(lambda k: to_x(k, EARLY))
    for k in range(2):
        for slot in (Y2, Z2):
            for rr in (r, other):
                arrived(slot, rr, k)
        for e in LATE:
            product(e, k)
    branches(lambda k: to_core(k, LATE))
    branches(lambda k: to_x(k, LATE))
    branches(lambda k: to_final(k, EARLY))
    branches(lambda k: to_final(k, LATE))

    local = ((0, 1), (0,), (), ())

    def finish(k):
        for dz in range(4):
            if dz not in local[k]:
                for n in range(2):
                    ref = outb.at[(z + dz) % 4, n]
                    pltpu.make_async_copy(ref, ref, f_r.at[(z + dz) % 4, n]).wait()

    branches(finish)
    for i in range(8):
        o_ref[:, i * rows : (i + 1) * rows] = outb[i // 2, i % 2]

    for cp in done:
        cp.wait_send()

    def drain(k):
        for e in PARITY[1 - k % 2]:
            core_copy(k, e).wait_send()
        for e, i, kind in x_moves(k, EARLY + LATE):
            x_copy(e, i, kind).wait_send()
        for e in QUARTER[k]:
            for cp in final_copies(k, e):
                cp.wait_send()

    branches(drain)


def gram(momentum):
    rows, cols = momentum.shape
    half = cols // 2
    n_rows = rows * lax.axis_size("tp")
    most = max(len(s) for s in QUARTER)
    dma = pltpu.SemaphoreType.DMA
    return pl.pallas_call(
        functools.partial(kernel, float(n_rows)),
        out_shape=jax.ShapeDtypeStruct((rows, 8 * rows), F32),
        in_specs=[pl.BlockSpec(memory_space=pl.ANY)],
        out_specs=pl.BlockSpec(memory_space=pltpu.VMEM),
        scratch_shapes=[
            pltpu.VMEM((len(SLOTS), 2 * rows, half), BF16),
            pltpu.VMEM((rows, half), BF16),
            pltpu.VMEM((len(PAIRS), 2 * rows, 2 * rows), F32),
            pltpu.VMEM((5, 2 * rows, 2 * rows), F32),
            pltpu.VMEM((most, 3, rows, 2 * rows), BF16),
            pltpu.VMEM((most, 3, rows, 2 * rows), BF16),
            pltpu.VMEM((most, 2, rows, rows), F32),
            pltpu.VMEM((most, 2, rows, rows), F32),
            pltpu.VMEM((4, 2, rows, rows), F32),
            pltpu.VMEM((3, 8, 128), F32),
            pltpu.VMEM((8, 8, 128), F32),
            pltpu.VMEM((4, 8, 128), F32),
            pltpu.VMEM((4, 8, 128), F32),
            dma((cols // CHUNK,)),
            dma((24,)),
            dma((3, 8)),
            dma((4, 2, 2)),
            dma((len(SLOTS), 2, 2)),
            dma((2, 2, 2)),
            dma((2,)),
            dma((5,)),
            dma((5,)),
            dma((most, 3)),
            dma((most, 3)),
            dma((most, 4)),
            dma((4, 2)),
        ],
        compiler_params=pltpu.CompilerParams(
            collective_id=0, has_side_effects=True, vmem_limit_bytes=62 * 2**20
        ),
        cost_estimate=pl.CostEstimate(
            flops=2 * 10 * (2 * rows) ** 2 * half, bytes_accessed=4 * rows * (cols + 8 * rows), transcendentals=0
        ),
    )(momentum)


def solution(mesh):
    return jax.shard_map(gram, mesh=mesh, in_specs=(P("tp", "col"),), out_specs=P("tp", "col"), check_vma=False)
```

```python
import functools

import jax
import jax.numpy as jnp
from jax import lax
from jax.experimental import pallas as pl
from jax.experimental.pallas import tpu as pltpu
from jax.sharding import PartitionSpec as P

SLOTS = ((0, 0), (1, 0), (3, 0), (0, 1), (0, 3), (2, 0), (0, 2))
OWN, Y1, Y3, Z1, Z3, Y2, Z2 = range(7)
PAIRS = (
    (OWN, OWN, False),
    (OWN, Z1, True),
    (Z3, Z1, False),
    (OWN, Y1, True),
    (Z1, Y1, True),
    (Y1, Y3, False),
    (Z1, Y3, True),
    (Z2, Y3, True),
    (Y2, Z1, True),
    (Z2, Y2, False),
)
QUARTER = tuple(tuple(e for e, (_, b, _) in enumerate(PAIRS) if SLOTS[b][0] == q) for q in range(4))
PARITY = tuple(tuple(sorted(QUARTER[p] + QUARTER[p + 2])) for p in range(2))
MESH = pl.DeviceIdType.MESH
F32, BF16 = jnp.float32, jnp.bfloat16
CHUNK = 384


def kernel(
    factor, m_ref, o_ref,
    slots, xsend, acc, d2, xs, xr, fb, ftb, outb, part, g8, gy, gz,
    in_sem, ps_s, ps_r, gat_s, gat_r, fwd_s, xc_s, d2_s, d2_r, x_s, x_r, f_s, f_r,
):
    rows = m_ref.shape[0]
    half = m_ref.shape[1] // 2
    cut = (half // 2) // 256 * 256
    spans = ((0, cut), (cut, half - cut))
    t, c = lax.axis_index("tp"), lax.axis_index("col")
    y, z, r = t // 8, (t // 2) % 4, t % 2
    q = (c - y + 4) % 4
    per_half = half // CHUNK

    def at(dy=0, dz=0, xl=None, dc=0):
        xl = r if xl is None else xl
        return ((((y + dy) % 4) * 4 + (z + dz) % 4) * 2 + xl, (c + dc + 4) % 4)

    core_peer = (t, c + 1 - 2 * (c % 2))
    other = 1 - r

    loads = []
    for j in range(2 * per_half):
        dst = acc.at[j // 2, pl.ds((j % 2) * rows, rows), pl.ds(0, CHUNK)]
        loads.append(pltpu.make_async_copy(m_ref.at[:, pl.ds(j * CHUNK, CHUNK)], dst, in_sem.at[j]))
        loads[-1].start()

    bar = pltpu.get_barrier_semaphore()
    me8 = r * 4 + c

    def at8(i):
        return ((y * 4 + z) * 2 + i // 4, i % 4)

    greet = [at8((me8 + o) % 8) for o in range(1, 8)]
    greet += [at(dy=o) for o in range(1, 4)] + [at(dz=o) for o in range(1, 4)]
    greet += [at(dz=1, xl=other), at(dz=3, xl=other)]
    for dy, dc in ((1, 3), (3, 1), (2, 2)):
        greet += [at(dy=dy, xl=r, dc=dc), at(dy=dy, xl=other, dc=dc)]
    for dev in greet:
        pl.semaphore_signal(bar, inc=1, device_id=dev, device_id_type=MESH)

    total = jnp.zeros((8, CHUNK), F32)
    for j in range(2 * per_half):
        loads[j].wait()
        v = acc[j // 2, (j % 2) * rows : (j % 2 + 1) * rows, 0:CHUNK]
        total += jnp.sum((v * v).reshape(rows // 8, 8, CHUNK), axis=0)
    part[0] = total[:, 0:128] + total[:, 128:256] + total[:, 256:384]
    pl.semaphore_wait(bar, len(greet))
    done = []

    def share(stage, place, me, n, device):
        place[pl.ds(me, 1)] = part[stage][None]
        copies = []
        for o in range(1, n):
            i = 8 * stage + o
            copies.append(
                pltpu.make_async_remote_copy(
                    part.at[stage], place.at[me], ps_s.at[i], ps_r.at[stage, o],
                    device_id=device(o), device_id_type=MESH,
                )
            )
            copies[-1].start()
        for o in range(1, n):
            copies[o - 1].wait_recv()
        done.extend(copies)
        return jnp.sum(place[...], axis=0)

    part[1] = share(0, g8, me8, 8, lambda o: at8((me8 + o) % 8))
    part[2] = share(1, gy, y, 4, lambda o: at(dy=o))
    whole = share(2, gz, z, 4, lambda o: at(dz=o))
    total = jnp.sum(jnp.sum(whole, axis=0, keepdims=True), axis=1, keepdims=True)
    scale = 1.0 / (jnp.sqrt(total) + 1e-07)

    def normalize(which, n0, n1, store):
        for n in range(n0, n1):
            v = acc[which * (per_half // 2) + n // 2, (n % 2) * rows : (n % 2 + 1) * rows, 0:CHUNK]
            store(n, (v * scale).astype(BF16))

    mine = pl.ds(pl.multiple_of(r * rows, 16), rows)
    theirs = pl.ds(pl.multiple_of(other * rows, 16), rows)

    def to_own(n, v):
        slots[OWN, mine, n * CHUNK : (n + 1) * CHUNK] = v

    def to_send(n, v):
        xsend[:, n * CHUNK : (n + 1) * CHUNK] = v

    def unit(slot, rr, k):
        start = pl.ds(pl.multiple_of(rr * rows, 16), rows)
        return slots.at[slot, start, pl.ds(*spans[k])]

    direct = ((Y1, at(dy=3)), (Y3, at(dy=1)), (Z1, at(dz=3)), (Z3, at(dz=1)))

    def send_own(rr, second, k):
        for i, (slot, dev) in enumerate(direct):
            cp = pltpu.make_async_remote_copy(
                unit(OWN, rr, k), unit(slot, rr, k), gat_s.at[i, second, k], gat_r.at[slot, rr, k],
                device_id=dev, device_id_type=MESH,
            )
            cp.start()
            done.append(cp)

    def arrived(slot, rr, k):
        ref = unit(slot, rr, k)
        pltpu.make_async_copy(ref, ref, gat_r.at[slot, rr, k]).wait()

    def send_x(k):
        cp = pltpu.make_async_remote_copy(
            xsend.at[:, pl.ds(*spans[k])], unit(OWN, r, k), xc_s.at[k], gat_r.at[OWN, r, k],
            device_id=at(xl=other), device_id_type=MESH,
        )
        cp.start()
        done.append(cp)

    onward = {Y1: (0, Y2, at(dy=3)), Z1: (1, Z2, at(dz=3)), Y3: (0, Y2, at(dy=1)), Z3: (1, Z2, at(dz=1))}

    def forward(slot, rr, second, k):
        i, to, dev = onward[slot]
        cp = pltpu.make_async_remote_copy(
            unit(slot, rr, k), unit(to, rr, k), fwd_s.at[i, second, k], gat_r.at[to, rr, k],
            device_id=dev, device_id_type=MESH,
        )
        cp.start()
        done.append(cp)

    first_cut = -(-cut // CHUNK)
    normalize(r, 0, first_cut, to_own)
    send_own(r, 0, 0)
    normalize(other, 0, first_cut, to_send)
    send_x(0)
    normalize(other, first_cut, per_half, to_send)
    normalize(r, first_cut, per_half, to_own)

    tile = 192

    def product(e, k, rr=None):
        a, b, _ = PAIRS[e]
        cols = pl.ds(*spans[k])
        size = tile if rr is None else tile // 2
        base = 0 if rr is None else rr * rows
        n = 2 * rows // tile

        def step(i, _):
            here = pl.ds(pl.multiple_of(base + i * size, size), size)
            p = lax.dot_general(
                slots[a, here, cols], slots[b, :, cols], (((1,), (1,)), ((), ())), preferred_element_type=F32
            )
            if k == 0:
                acc[e, here, :] = p
            else:
                acc[e, here, :] += p
            return 0

        lax.fori_loop(0, n, step, 0)

    arrived(OWN, other, 0)
    send_x(1)
    send_own(other, 1, 0)
    send_own(r, 0, 1)
    arrived(OWN, other, 1)
    send_own(other, 1, 1)

    def branches(body):
        for k in range(4):
            @pl.when(q == k)
            def _(k=k):
                body(k)

    def core_copy(k, e):
        i = PARITY[1 - k % 2].index(e)
        return pltpu.make_async_remote_copy(
            acc.at[e], d2.at[i], d2_s.at[i], d2_r.at[i], device_id=core_peer, device_id_type=MESH
        )

    def to_core(e):
        def body(k):
            if e in PARITY[1 - k % 2]:
                core_copy(k, e).start()

        branches(body)

    def x_copy(e, i, kind):
        dev = (at(xl=other), at(dc=2), at(xl=other, dc=2))[kind]
        return pltpu.make_async_remote_copy(
            xs.at[i, kind], xr.at[i, kind], x_s.at[i, kind], x_r.at[i, kind], device_id=dev, device_id_type=MESH
        )

    def x_moves(k, e):
        if e in QUARTER[k]:
            return [(QUARTER[k].index(e), 0)]
        i = QUARTER[(k + 2) % 4].index(e)
        return [(i, 1), (i, 2)]

    short = rows // 2

    def band(rr, n):
        return pl.ds(pl.multiple_of(rr * rows + n * short, 16), short)

    def to_x(e):
        def body(k):
            if e not in PARITY[k % 2]:
                return
            j = PARITY[k % 2].index(e)
            pltpu.make_async_copy(d2.at[j], d2.at[j], d2_r.at[j]).wait()
            for i, kind in x_moves(k, e):
                rr = r if kind == 1 else other
                for n in range(2):
                    v = acc[e, band(rr, n), :] + d2[j, band(rr, n), :]
                    xs[i, kind, :, n * 2 * rows : (n + 1) * 2 * rows] = v.astype(BF16)
                x_copy(e, i, kind).start()

        branches(body)

    def final_copies(k, e):
        a, b, both = PAIRS[e]
        i = QUARTER[k].index(e)
        (ay, az), (by, bz) = SLOTS[a], SLOTS[b]
        copies = []
        if a != OWN:
            for n in range(2):
                copies.append(
                    pltpu.make_async_remote_copy(
                        fb.at[i, n], outb.at[(z + bz) % 4, n], f_s.at[i, n], f_r.at[(z + bz) % 4, n],
                        device_id=at(ay, az), device_id_type=MESH,
                    )
                )
        if both:
            for n in range(2):
                copies.append(
                    pltpu.make_async_remote_copy(
                        ftb.at[i, n], outb.at[(z + az) % 4, r], f_s.at[i, 2 + n], f_r.at[(z + az) % 4, r],
                        device_id=at(by, bz, xl=n, dc=ay - by), device_id_type=MESH,
                    )
                )
        return copies

    quart = rows // 4

    def fold(ref, v, first=0):
        for n in range(v.shape[0] // quart):
            ref[:, (first + n) * rows : (first + n + 1) * rows] = v[n * quart : (n + 1) * quart]

    def to_final(e):
        def body(k):
            if e not in QUARTER[k]:
                return
            a, b, both = PAIRS[e]
            i = QUARTER[k].index(e)
            j = PARITY[k % 2].index(e)
            for kind in range(3):
                pltpu.make_async_copy(xr.at[i, kind], xr.at[i, kind], x_r.at[i, kind]).wait()
            parts = []
            for n in range(2):
                v = acc[e, band(r, n), :] + d2[j, band(r, n), :]
                for kind in range(3):
                    v += xr[i, kind, :, n * 2 * rows : (n + 1) * 2 * rows].astype(F32)
                parts.append(v * factor)
            bz = SLOTS[b][1]
            for n in range(2):
                w = [v[:, n * rows : (n + 1) * rows] for v in parts]
                ref = outb.at[(z + bz) % 4, n] if a == OWN else fb.at[i, n]
                fold(ref, w[0])
                fold(ref, w[1], 2)
                if both:
                    fold(ftb.at[i, n], jnp.concatenate(w, axis=0).T)
            for cp in final_copies(k, e):
                cp.start()

        branches(body)

    for k in range(2):
        product(0, k)
    to_core(0)
    for slot in (Y1, Z1, Y3, Z3):
        for rr in (r, other):
            arrived(slot, rr, 0)
    to_x(0)
    early = (4, 6, 3, 5, 1, 2)
    for e in early:
        product(e, 0)
    for slot in (Y1, Z1, Y3, Z3):
        for rr in (r, other):
            arrived(slot, rr, 1)
    for n, rr in enumerate((r, other)):
        for slot in (Y1, Z1):
            forward(slot, rr, n, 0)
        for slot in (Y3, Z3):
            forward(slot, rr, n, 1)
    for n, e in enumerate(early):
        product(e, 1)
        to_core(e)
        if n:
            to_x(early[n - 1])
    to_x(early[-1])
    to_final(0)
    for rr in (r, other):
        for slot in (Z2, Y2):
            for k in range(2):
                arrived(slot, rr, k)
        for e in (7, 8):
            for k in range(2):
                product(e, k, rr)
    to_core(7)
    to_core(8)
    for k in range(2):
        product(9, k)
    to_core(9)
    for e in (7, 8, 9):
        to_x(e)
    for e in early + (7, 8, 9):
        to_final(e)

    local = ((0, 1), (0,), (), ())

    def finish(k):
        for dz in range(4):
            if dz not in local[k]:
                for n in range(2):
                    ref = outb.at[(z + dz) % 4, n]
                    pltpu.make_async_copy(ref, ref, f_r.at[(z + dz) % 4, n]).wait()

    branches(finish)
    for i in range(8):
        for n in range(4):
            o_ref[n * quart : (n + 1) * quart, i * rows : (i + 1) * rows] = outb[
                i // 2, i % 2, :, n * rows : (n + 1) * rows
            ]

    for cp in done:
        cp.wait_send()

    def drain(k):
        for e in PARITY[1 - k % 2]:
            core_copy(k, e).wait_send()
        for e in PARITY[k % 2]:
            for i, kind in x_moves(k, e):
                x_copy(e, i, kind).wait_send()
        for e in QUARTER[k]:
            for cp in final_copies(k, e):
                cp.wait_send()

    branches(drain)


def gram(momentum):
    rows, cols = momentum.shape
    half = cols // 2
    n_rows = rows * lax.axis_size("tp")
    most = max(len(s) for s in QUARTER)
    dma = pltpu.SemaphoreType.DMA
    return pl.pallas_call(
        functools.partial(kernel, float(n_rows)),
        out_shape=jax.ShapeDtypeStruct((rows, 8 * rows), F32),
        in_specs=[pl.BlockSpec(memory_space=pl.ANY)],
        out_specs=pl.BlockSpec(memory_space=pltpu.VMEM),
        scratch_shapes=[
            pltpu.VMEM((len(SLOTS), 2 * rows, half), BF16),
            pltpu.VMEM((rows, half), BF16),
            pltpu.VMEM((len(PAIRS), 2 * rows, 2 * rows), F32),
            pltpu.VMEM((5, 2 * rows, 2 * rows), F32),
            pltpu.VMEM((most, 3, rows // 2, 4 * rows), BF16),
            pltpu.VMEM((most, 3, rows // 2, 4 * rows), BF16),
            pltpu.VMEM((most, 2, rows // 4, 4 * rows), F32),
            pltpu.VMEM((most, 2, rows // 4, 4 * rows), F32),
            pltpu.VMEM((4, 2, rows // 4, 4 * rows), F32),
            pltpu.VMEM((3, 8, 128), F32),
            pltpu.VMEM((8, 8, 128), F32),
            pltpu.VMEM((4, 8, 128), F32),
            pltpu.VMEM((4, 8, 128), F32),
            dma((cols // CHUNK,)),
            dma((24,)),
            dma((3, 8)),
            dma((4, 2, 2)),
            dma((len(SLOTS), 2, 2)),
            dma((2, 2, 2)),
            dma((2,)),
            dma((5,)),
            dma((5,)),
            dma((most, 3)),
            dma((most, 3)),
            dma((most, 4)),
            dma((4, 2)),
        ],
        compiler_params=pltpu.CompilerParams(
            collective_id=0, has_side_effects=True, vmem_limit_bytes=62 * 2**20
        ),
        cost_estimate=pl.CostEstimate(
            flops=2 * 10 * (2 * rows) ** 2 * half, bytes_accessed=4 * rows * (cols + 8 * rows), transcendentals=0
        ),
    )(momentum)


def solution(mesh):
    return jax.shard_map(gram, mesh=mesh, in_specs=(P("tp", "col"),), out_specs=P("tp", "col"), check_vma=False)
```

```python
import functools

import jax
import jax.numpy as jnp
from jax import lax
from jax.experimental import pallas as pl
from jax.experimental.pallas import tpu as pltpu
from jax.sharding import PartitionSpec as P

SLOTS = ((0, 0), (1, 0), (3, 0), (0, 1), (0, 3), (2, 0), (0, 2))
OWN, Y1, Y3, Z1, Z3, Y2, Z2 = range(7)
PAIRS = (
    (OWN, OWN, False, 0),
    (OWN, Z1, True, 0),
    (Z3, Z1, False, 2),
    (OWN, Y1, True, 1),
    (Z1, Y1, True, 1),
    (Y1, Y3, False, 3),
    (Z1, Y3, True, 3),
    (Z2, Y3, True, 3),
    (Z1, Y2, True, 2),
    (Y2, Z2, False, 0),
)
QUARTER = tuple(tuple(e for e, p in enumerate(PAIRS) if p[3] == q) for q in range(4))
PARITY = tuple(tuple(sorted(QUARTER[p] + QUARTER[p + 2])) for p in range(2))
SENT = tuple(tuple(e for e in q if e) for q in QUARTER)
MESH = pl.DeviceIdType.MESH
F32, BF16 = jnp.float32, jnp.bfloat16
CHUNK = 384


def kernel(
    factor, m_ref, o_ref,
    slots, xsend, acc, d2, xs, xr, fb, ftb, got, outb, part, g8, gy, gz,
    in_sem, ps_s, ps_r, gat_s, gat_r, fwd_s, xc_s, d2_s, d2_r, x_s, x_r, f_s, f_r,
):
    rows = m_ref.shape[0]
    half = m_ref.shape[1] // 2
    cut = (half // 2) // 256 * 256
    spans = ((0, cut), (cut, half - cut))
    t, c = lax.axis_index("tp"), lax.axis_index("col")
    y, z, r = t // 8, (t // 2) % 4, t % 2
    q = (c - y + 4) % 4
    per_half = half // CHUNK

    def at(dy=0, dz=0, xl=None, dc=0):
        xl = r if xl is None else xl
        return ((((y + dy) % 4) * 4 + (z + dz) % 4) * 2 + xl, (c + dc + 4) % 4)

    core_peer = (t, c + 1 - 2 * (c % 2))
    other = 1 - r

    loads = []
    for j in range(2 * per_half):
        dst = acc.at[j // 2, pl.ds((j % 2) * rows, rows), pl.ds(0, CHUNK)]
        loads.append(pltpu.make_async_copy(m_ref.at[:, pl.ds(j * CHUNK, CHUNK)], dst, in_sem.at[j]))
        loads[-1].start()

    bar = pltpu.get_barrier_semaphore()
    me8 = r * 4 + c

    def at8(i):
        return ((y * 4 + z) * 2 + i // 4, i % 4)

    greet = [at8((me8 + o) % 8) for o in range(1, 8)]
    greet += [at(dy=o) for o in range(1, 4)] + [at(dz=o) for o in range(1, 4)]
    greet += [at(dz=1, xl=other), at(dz=3, xl=other), at(dz=1, dc=2), at(dz=3, dc=2)]
    for dy, dc in ((1, 3), (3, 1), (2, 2)):
        greet += [at(dy=dy, xl=r, dc=dc), at(dy=dy, xl=other, dc=dc)]
    for dev in greet:
        pl.semaphore_signal(bar, inc=1, device_id=dev, device_id_type=MESH)

    total = jnp.zeros((8, CHUNK), F32)
    for j in range(2 * per_half):
        loads[j].wait()
        v = acc[j // 2, (j % 2) * rows : (j % 2 + 1) * rows, 0:CHUNK]
        total += jnp.sum((v * v).reshape(rows // 8, 8, CHUNK), axis=0)
    part[0] = total[:, 0:128] + total[:, 128:256] + total[:, 256:384]
    pl.semaphore_wait(bar, len(greet))
    done = []

    def share(stage, place, me, n, device):
        place[pl.ds(me, 1)] = part[stage][None]
        copies = []
        for o in range(1, n):
            i = 8 * stage + o
            copies.append(
                pltpu.make_async_remote_copy(
                    part.at[stage], place.at[me], ps_s.at[i], ps_r.at[stage, o],
                    device_id=device(o), device_id_type=MESH,
                )
            )
            copies[-1].start()
        for o in range(1, n):
            copies[o - 1].wait_recv()
        done.extend(copies)
        return jnp.sum(place[...], axis=0)

    part[1] = share(0, g8, me8, 8, lambda o: at8((me8 + o) % 8))
    part[2] = share(1, gy, y, 4, lambda o: at(dy=o))
    whole = share(2, gz, z, 4, lambda o: at(dz=o))
    total = jnp.sum(jnp.sum(whole, axis=0, keepdims=True), axis=1, keepdims=True)
    scale = 1.0 / (jnp.sqrt(total) + 1e-07)

    def normalize(which, n0, n1, store):
        for n in range(n0, n1):
            v = acc[which * (per_half // 2) + n // 2, (n % 2) * rows : (n % 2 + 1) * rows, 0:CHUNK]
            store(n, (v * scale).astype(BF16))

    mine = pl.ds(pl.multiple_of(r * rows, 16), rows)
    theirs = pl.ds(pl.multiple_of(other * rows, 16), rows)

    def to_own(n, v):
        slots[OWN, mine, n * CHUNK : (n + 1) * CHUNK] = v

    def to_send(n, v):
        xsend[:, n * CHUNK : (n + 1) * CHUNK] = v

    def unit(slot, rr, k):
        start = pl.ds(pl.multiple_of(rr * rows, 16), rows)
        return slots.at[slot, start, pl.ds(*spans[k])]

    direct = ((Y1, at(dy=3)), (Y3, at(dy=1)), (Z1, at(dz=3)), (Z3, at(dz=1)))

    def send_own(rr, second, k):
        for i, (slot, dev) in enumerate(direct):
            cp = pltpu.make_async_remote_copy(
                unit(OWN, rr, k), unit(slot, rr, k), gat_s.at[i, second, k], gat_r.at[slot, rr, k],
                device_id=dev, device_id_type=MESH,
            )
            cp.start()
            done.append(cp)

    def arrived(slot, rr, k):
        ref = unit(slot, rr, k)
        pltpu.make_async_copy(ref, ref, gat_r.at[slot, rr, k]).wait()

    def send_x(k):
        cp = pltpu.make_async_remote_copy(
            xsend.at[:, pl.ds(*spans[k])], unit(OWN, r, k), xc_s.at[k], gat_r.at[OWN, r, k],
            device_id=at(xl=other), device_id_type=MESH,
        )
        cp.start()
        done.append(cp)

    onward = {Y1: (0, Y2, at(dy=3)), Z1: (1, Z2, at(dz=3)), Y3: (0, Y2, at(dy=1)), Z3: (1, Z2, at(dz=1))}

    def forward(slot, rr, second, k):
        i, to, dev = onward[slot]
        cp = pltpu.make_async_remote_copy(
            unit(slot, rr, k), unit(to, rr, k), fwd_s.at[i, second, k], gat_r.at[to, rr, k],
            device_id=dev, device_id_type=MESH,
        )
        cp.start()
        done.append(cp)

    first_cut = -(-cut // CHUNK)
    normalize(r, 0, first_cut, to_own)
    send_own(r, 0, 0)
    normalize(other, 0, first_cut, to_send)
    send_x(0)
    normalize(other, first_cut, per_half, to_send)
    normalize(r, first_cut, per_half, to_own)

    tile = 192

    def product(e, k, rr=None):
        a, b = PAIRS[e][:2]
        cols = pl.ds(*spans[k])
        size = tile if rr is None else tile // 2
        base = 0 if rr is None else rr * rows
        n = 2 * rows // tile

        def step(i, _):
            here = pl.ds(pl.multiple_of(base + i * size, size), size)
            p = lax.dot_general(
                slots[a, here, cols], slots[b, :, cols], (((1,), (1,)), ((), ())), preferred_element_type=F32
            )
            if k == 0:
                acc[e, here, :] = p
            else:
                acc[e, here, :] += p
            return 0

        lax.fori_loop(0, n, step, 0)

    arrived(OWN, other, 0)
    send_x(1)
    send_own(other, 1, 0)
    send_own(r, 0, 1)
    arrived(OWN, other, 1)
    send_own(other, 1, 1)

    def branches(body):
        for k in range(4):
            @pl.when(q == k)
            def _(k=k):
                body(k)

    def core_copy(k, e):
        i = PARITY[1 - k % 2].index(e)
        return pltpu.make_async_remote_copy(
            acc.at[e], d2.at[i], d2_s.at[i], d2_r.at[i], device_id=core_peer, device_id_type=MESH
        )

    def to_core(e):
        def body(k):
            if e in PARITY[1 - k % 2]:
                core_copy(k, e).start()

        branches(body)

    def x_copy(e, i, kind):
        dev = (at(xl=other), at(dc=2), at(xl=other, dc=2))[kind]
        return pltpu.make_async_remote_copy(
            xs.at[i, kind], xr.at[i, kind], x_s.at[i, kind], x_r.at[i, kind], device_id=dev, device_id_type=MESH
        )

    def x_moves(k, e):
        if e in QUARTER[k]:
            return [(QUARTER[k].index(e), 0)]
        i = QUARTER[(k + 2) % 4].index(e)
        return [(i, 1), (i, 2)]

    short = rows // 2

    def band(rr, n):
        return pl.ds(pl.multiple_of(rr * rows + n * short, 16), short)

    def to_x(e):
        def body(k):
            if e not in PARITY[k % 2]:
                return
            j = PARITY[k % 2].index(e)
            pltpu.make_async_copy(d2.at[j], d2.at[j], d2_r.at[j]).wait()
            for i, kind in x_moves(k, e):
                rr = r if kind == 1 else other
                for n in range(2):
                    v = acc[e, band(rr, n), :] + d2[j, band(rr, n), :]
                    xs[i, kind, :, n * 2 * rows : (n + 1) * 2 * rows] = v.astype(BF16)
                x_copy(e, i, kind).start()

        branches(body)

    def final_copies(k, e):
        a, b, both, q_e = PAIRS[e]
        i = SENT[k].index(e)
        (ay, az), (by, bz) = SLOTS[a], SLOTS[b]
        copies = []
        if a != OWN:
            for n in range(2):
                copies.append(
                    pltpu.make_async_remote_copy(
                        fb.at[i, n], got.at[(z + bz) % 4, n], f_s.at[i, n], f_r.at[(z + bz) % 4, n],
                        device_id=at(ay, az, dc=by - q_e), device_id_type=MESH,
                    )
                )
        if both:
            for n in range(2):
                copies.append(
                    pltpu.make_async_remote_copy(
                        ftb.at[i, n], got.at[(z + az) % 4, r], f_s.at[i, 2 + n], f_r.at[(z + az) % 4, r],
                        device_id=at(by, bz, xl=n, dc=ay - q_e), device_id_type=MESH,
                    )
                )
        return copies

    quart = rows // 4

    def fold(ref, w):
        for m in range(4):
            ref[:, m * rows : (m + 1) * rows] = w[m // 2][(m % 2) * quart : (m % 2 + 1) * quart]

    def pair_up(ref, w):
        for m in range(2):
            ref[:, m * rows : (m + 1) * rows] = w[m].astype(BF16)

    def to_final(e):
        def body(k):
            if e not in QUARTER[k]:
                return
            a, b, both, _ = PAIRS[e]
            i = QUARTER[k].index(e)
            j = PARITY[k % 2].index(e)
            for kind in range(3):
                pltpu.make_async_copy(xr.at[i, kind], xr.at[i, kind], x_r.at[i, kind]).wait()
            parts = []
            for n in range(2):
                v = acc[e, band(r, n), :] + d2[j, band(r, n), :]
                for kind in range(3):
                    v += xr[i, kind, :, n * 2 * rows : (n + 1) * 2 * rows].astype(F32)
                parts.append(v * factor)
            bz = SLOTS[b][1]
            f = SENT[k].index(e) if e else None
            for n in range(2):
                w = [v[:, n * rows : (n + 1) * rows] for v in parts]
                if a == OWN:
                    fold(outb.at[(z + bz) % 4, n], w)
                else:
                    pair_up(fb.at[f, n], w)
                if both:
                    turned = jnp.concatenate(w, axis=0).T
                    pair_up(ftb.at[f, n], (turned[:short], turned[short:]))
            if e:
                for cp in final_copies(k, e):
                    cp.start()

        branches(body)

    for k in range(2):
        product(0, k)
    to_core(0)
    for slot in (Y1, Z1, Y3, Z3):
        for rr in (r, other):
            arrived(slot, rr, 0)
    to_x(0)
    early = (4, 6, 3, 5, 1, 2)
    for e in early:
        product(e, 0)
    for slot in (Y1, Z1, Y3, Z3):
        for rr in (r, other):
            arrived(slot, rr, 1)
    for n, rr in enumerate((r, other)):
        for slot in (Y1, Z1):
            forward(slot, rr, n, 0)
        for slot in (Y3, Z3):
            forward(slot, rr, n, 1)
    for n, e in enumerate(early):
        product(e, 1)
        to_core(e)
        if n:
            to_x(early[n - 1])
    to_x(early[-1])
    to_final(0)
    for rr in (r, other):
        for k in range(2):
            arrived(Z2, rr, k)
        for k in range(2):
            product(7, k, rr)
    to_core(7)
    for k in range(2):
        for rr in (r, other):
            arrived(Y2, rr, k)
        product(8, k)
    to_core(8)
    to_x(7)
    for k in range(2):
        product(9, k)
    to_core(9)
    to_x(8)
    to_x(9)
    for e in early + (7, 8, 9):
        to_final(e)

    local = ((0, 1), (0,), (), ())

    def finish(k):
        for dz in range(4):
            if dz in local[k]:
                continue
            for n in range(2):
                ref = got.at[(z + dz) % 4, n]
                pltpu.make_async_copy(ref, ref, f_r.at[(z + dz) % 4, n]).wait()
                v = ref[...].astype(F32)
                fold(outb.at[(z + dz) % 4, n], (v[:, 0:rows], v[:, rows : 2 * rows]))

    branches(finish)
    for i in range(8):
        for n in range(4):
            o_ref[n * quart : (n + 1) * quart, i * rows : (i + 1) * rows] = outb[
                i // 2, i % 2, :, n * rows : (n + 1) * rows
            ]

    for cp in done:
        cp.wait_send()

    def drain(k):
        for e in PARITY[1 - k % 2]:
            core_copy(k, e).wait_send()
        for e in PARITY[k % 2]:
            for i, kind in x_moves(k, e):
                x_copy(e, i, kind).wait_send()
        for e in QUARTER[k]:
            if e:
                for cp in final_copies(k, e):
                    cp.wait_send()

    branches(drain)


def gram(momentum):
    rows, cols = momentum.shape
    half = cols // 2
    n_rows = rows * lax.axis_size("tp")
    most = max(len(s) for s in QUARTER)
    sent = max(len(s) for s in SENT)
    dma = pltpu.SemaphoreType.DMA
    return pl.pallas_call(
        functools.partial(kernel, float(n_rows)),
        out_shape=jax.ShapeDtypeStruct((rows, 8 * rows), F32),
        in_specs=[pl.BlockSpec(memory_space=pl.ANY)],
        out_specs=pl.BlockSpec(memory_space=pltpu.VMEM),
        scratch_shapes=[
            pltpu.VMEM((len(SLOTS), 2 * rows, half), BF16),
            pltpu.VMEM((rows, half), BF16),
            pltpu.VMEM((len(PAIRS), 2 * rows, 2 * rows), F32),
            pltpu.VMEM((5, 2 * rows, 2 * rows), F32),
            pltpu.VMEM((most, 3, rows // 2, 4 * rows), BF16),
            pltpu.VMEM((most, 3, rows // 2, 4 * rows), BF16),
            pltpu.VMEM((sent, 2, rows // 2, 2 * rows), BF16),
            pltpu.VMEM((sent, 2, rows // 2, 2 * rows), BF16),
            pltpu.VMEM((4, 2, rows // 2, 2 * rows), BF16),
            pltpu.VMEM((4, 2, rows // 4, 4 * rows), F32),
            pltpu.VMEM((3, 8, 128), F32),
            pltpu.VMEM((8, 8, 128), F32),
            pltpu.VMEM((4, 8, 128), F32),
            pltpu.VMEM((4, 8, 128), F32),
            dma((cols // CHUNK,)),
            dma((24,)),
            dma((3, 8)),
            dma((4, 2, 2)),
            dma((len(SLOTS), 2, 2)),
            dma((2, 2, 2)),
            dma((2,)),
            dma((5,)),
            dma((5,)),
            dma((most, 3)),
            dma((most, 3)),
            dma((sent, 4)),
            dma((4, 2)),
        ],
        compiler_params=pltpu.CompilerParams(
            collective_id=0, has_side_effects=True, vmem_limit_bytes=62 * 2**20
        ),
        cost_estimate=pl.CostEstimate(
            flops=2 * 10 * (2 * rows) ** 2 * half, bytes_accessed=4 * rows * (cols + 8 * rows), transcendentals=0
        ),
    )(momentum)


def solution(mesh):
    return jax.shard_map(gram, mesh=mesh, in_specs=(P("tp", "col"),), out_specs=P("tp", "col"), check_vma=False)
```

```python
import functools

import jax
import jax.numpy as jnp
from jax import lax
from jax.experimental import pallas as pl
from jax.experimental.pallas import tpu as pltpu
from jax.sharding import PartitionSpec as P

SLOTS = ((0, 0), (1, 0), (3, 0), (0, 1), (0, 3), (2, 0), (0, 2))
OWN, Y1, Y3, Z1, Z3, Y2, Z2 = range(7)
PAIRS = (
    (OWN, OWN, False, 0),
    (OWN, Z1, True, 0),
    (Z3, Z1, False, 2),
    (OWN, Y1, True, 1),
    (Z1, Y1, True, 1),
    (Y1, Y3, False, 3),
    (Z1, Y3, True, 3),
    (Z2, Y3, True, 3),
    (Z1, Y2, True, 2),
    (Y2, Z2, False, 0),
)
QUARTER = tuple(tuple(e for e, p in enumerate(PAIRS) if p[3] == q) for q in range(4))
PARITY = tuple(tuple(sorted(QUARTER[p] + QUARTER[p + 2])) for p in range(2))
SENT = tuple(tuple(e for e in q if e) for q in QUARTER)
MESH = pl.DeviceIdType.MESH
F32, BF16 = jnp.float32, jnp.bfloat16
CHUNK = 384


def kernel(
    factor, m_ref, o_ref,
    slots, xsend, acc, d2, xs, xr, fb, ftb, got, outb, part, g8, gy, gz,
    in_sem, ps_s, ps_r, gat_s, gat_r, fwd_s, xc_s, d2_s, d2_r, x_s, x_r, f_s, f_r,
):
    rows = m_ref.shape[0]
    half = m_ref.shape[1] // 2
    cut = (half // 2) // 256 * 256
    spans = ((0, cut), (cut, half - cut))
    t, c = lax.axis_index("tp"), lax.axis_index("col")
    y, z, r = t // 8, (t // 2) % 4, t % 2
    q = (c - y + 4) % 4
    per_half = half // CHUNK

    def at(dy=0, dz=0, xl=None, dc=0):
        xl = r if xl is None else xl
        return ((((y + dy) % 4) * 4 + (z + dz) % 4) * 2 + xl, (c + dc + 4) % 4)

    core_peer = (t, c + 1 - 2 * (c % 2))
    other = 1 - r

    loads = []
    for j in range(2 * per_half):
        dst = acc.at[j // 2, pl.ds((j % 2) * rows, rows), pl.ds(0, CHUNK)]
        loads.append(pltpu.make_async_copy(m_ref.at[:, pl.ds(j * CHUNK, CHUNK)], dst, in_sem.at[j]))
        loads[-1].start()

    bar = pltpu.get_barrier_semaphore()
    me8 = r * 4 + c

    def at8(i):
        return ((y * 4 + z) * 2 + i // 4, i % 4)

    greet = [at8((me8 + o) % 8) for o in range(1, 8)]
    greet += [at(dy=o) for o in range(1, 4)] + [at(dz=o) for o in range(1, 4)]
    greet += [at(dz=1, xl=other), at(dz=3, xl=other), at(dz=1, dc=2), at(dz=3, dc=2)]
    for dy, dc in ((1, 3), (3, 1), (2, 2)):
        greet += [at(dy=dy, xl=r, dc=dc), at(dy=dy, xl=other, dc=dc)]
    for dev in greet:
        pl.semaphore_signal(bar, inc=1, device_id=dev, device_id_type=MESH)

    total = jnp.zeros((8, CHUNK), F32)
    for j in range(2 * per_half):
        loads[j].wait()
        v = acc[j // 2, (j % 2) * rows : (j % 2 + 1) * rows, 0:CHUNK]
        total += jnp.sum((v * v).reshape(rows // 8, 8, CHUNK), axis=0)
    part[0] = total[:, 0:128] + total[:, 128:256] + total[:, 256:384]
    pl.semaphore_wait(bar, len(greet))
    done = []

    def share(stage, place, me, n, device):
        place[pl.ds(me, 1)] = part[stage][None]
        copies = []
        for o in range(1, n):
            i = 8 * stage + o
            copies.append(
                pltpu.make_async_remote_copy(
                    part.at[stage], place.at[me], ps_s.at[i], ps_r.at[stage, o],
                    device_id=device(o), device_id_type=MESH,
                )
            )
            copies[-1].start()
        for o in range(1, n):
            copies[o - 1].wait_recv()
        done.extend(copies)
        return jnp.sum(place[...], axis=0)

    part[1] = share(0, g8, me8, 8, lambda o: at8((me8 + o) % 8))
    part[2] = share(1, gy, y, 4, lambda o: at(dy=o))
    whole = share(2, gz, z, 4, lambda o: at(dz=o))
    total = jnp.sum(jnp.sum(whole, axis=0, keepdims=True), axis=1, keepdims=True)
    scale = 1.0 / (jnp.sqrt(total) + 1e-07)

    def normalize(which, n0, n1, store):
        for n in range(n0, n1):
            v = acc[which * (per_half // 2) + n // 2, (n % 2) * rows : (n % 2 + 1) * rows, 0:CHUNK]
            store(n, (v * scale).astype(BF16))

    mine = pl.ds(pl.multiple_of(r * rows, 16), rows)
    theirs = pl.ds(pl.multiple_of(other * rows, 16), rows)

    def to_own(n, v):
        slots[OWN, mine, n * CHUNK : (n + 1) * CHUNK] = v

    def to_send(n, v):
        xsend[:, n * CHUNK : (n + 1) * CHUNK] = v

    def unit(slot, rr, k):
        start = pl.ds(pl.multiple_of(rr * rows, 16), rows)
        return slots.at[slot, start, pl.ds(*spans[k])]

    direct = ((Y1, at(dy=3)), (Y3, at(dy=1)), (Z1, at(dz=3)), (Z3, at(dz=1)))

    def send_own(rr, second, k):
        for i, (slot, dev) in enumerate(direct):
            cp = pltpu.make_async_remote_copy(
                unit(OWN, rr, k), unit(slot, rr, k), gat_s.at[i, second, k], gat_r.at[slot, rr, k],
                device_id=dev, device_id_type=MESH,
            )
            cp.start()
            done.append(cp)

    def arrived(slot, rr, k):
        ref = unit(slot, rr, k)
        pltpu.make_async_copy(ref, ref, gat_r.at[slot, rr, k]).wait()

    def send_x(k):
        cp = pltpu.make_async_remote_copy(
            xsend.at[:, pl.ds(*spans[k])], unit(OWN, r, k), xc_s.at[k], gat_r.at[OWN, r, k],
            device_id=at(xl=other), device_id_type=MESH,
        )
        cp.start()
        done.append(cp)

    onward = {Y1: (0, Y2, at(dy=3)), Z1: (1, Z2, at(dz=3)), Y3: (0, Y2, at(dy=1)), Z3: (1, Z2, at(dz=1))}

    def forward(slot, rr, second, k):
        i, to, dev = onward[slot]
        cp = pltpu.make_async_remote_copy(
            unit(slot, rr, k), unit(to, rr, k), fwd_s.at[i, second, k], gat_r.at[to, rr, k],
            device_id=dev, device_id_type=MESH,
        )
        cp.start()
        done.append(cp)

    first_cut = -(-cut // CHUNK)
    normalize(r, 0, first_cut, to_own)
    send_own(r, 0, 0)
    normalize(other, 0, first_cut, to_send)
    send_x(0)
    normalize(other, first_cut, per_half, to_send)
    normalize(r, first_cut, per_half, to_own)

    tile = 192

    def product(e, k, rr=None):
        a, b = PAIRS[e][:2]
        cols = pl.ds(*spans[k])
        size = tile if rr is None else tile // 2
        base = 0 if rr is None else rr * rows
        n = 2 * rows // tile

        def step(i, _):
            here = pl.ds(pl.multiple_of(base + i * size, size), size)
            p = lax.dot_general(
                slots[a, here, cols], slots[b, :, cols], (((1,), (1,)), ((), ())), preferred_element_type=F32
            )
            if k == 0:
                acc[e, here, :] = p
            else:
                acc[e, here, :] += p
            return 0

        lax.fori_loop(0, n, step, 0)

    arrived(OWN, other, 0)
    send_x(1)
    send_own(other, 1, 0)
    send_own(r, 0, 1)
    arrived(OWN, other, 1)
    send_own(other, 1, 1)

    def branches(body):
        for k in range(4):
            @pl.when(q == k)
            def _(k=k):
                body(k)

    def core_copy(k, e):
        i = PARITY[1 - k % 2].index(e)
        return pltpu.make_async_remote_copy(
            acc.at[e], d2.at[i], d2_s.at[i], d2_r.at[i], device_id=core_peer, device_id_type=MESH
        )

    def to_core(e):
        def body(k):
            if e in PARITY[1 - k % 2]:
                core_copy(k, e).start()

        branches(body)

    def x_copy(e, i, kind):
        dev = (at(xl=other), at(dc=2), at(xl=other, dc=2))[kind]
        return pltpu.make_async_remote_copy(
            xs.at[i, kind], xr.at[i, kind], x_s.at[i, kind], x_r.at[i, kind], device_id=dev, device_id_type=MESH
        )

    def x_moves(k, e):
        if e in QUARTER[k]:
            return [(QUARTER[k].index(e), 0)]
        i = QUARTER[(k + 2) % 4].index(e)
        return [(i, 1), (i, 2)]

    short = rows // 2

    def band(rr, n):
        return pl.ds(pl.multiple_of(rr * rows + n * short, 16), short)

    def to_x(e):
        def body(k):
            if e not in PARITY[k % 2]:
                return
            j = PARITY[k % 2].index(e)
            pltpu.make_async_copy(d2.at[j], d2.at[j], d2_r.at[j]).wait()
            for i, kind in x_moves(k, e):
                rr = r if kind == 1 else other
                for n in range(2):
                    v = acc[e, band(rr, n), :] + d2[j, band(rr, n), :]
                    xs[i, kind, :, n * 2 * rows : (n + 1) * 2 * rows] = v.astype(BF16)
                x_copy(e, i, kind).start()

        branches(body)

    def final_copies(k, e):
        a, b, both, q_e = PAIRS[e]
        i = SENT[k].index(e)
        (ay, az), (by, bz) = SLOTS[a], SLOTS[b]
        copies = []
        if a != OWN:
            for n in range(2):
                copies.append(
                    pltpu.make_async_remote_copy(
                        fb.at[i, n], got.at[(z + bz) % 4, n], f_s.at[i, n], f_r.at[(z + bz) % 4, n],
                        device_id=at(ay, az, dc=by - q_e), device_id_type=MESH,
                    )
                )
        if both:
            for n in range(2):
                copies.append(
                    pltpu.make_async_remote_copy(
                        ftb.at[i, n], got.at[(z + az) % 4, r], f_s.at[i, 2 + n], f_r.at[(z + az) % 4, r],
                        device_id=at(by, bz, xl=n, dc=ay - q_e), device_id_type=MESH,
                    )
                )
        return copies

    quart = rows // 4

    def fold(ref, w):
        for m in range(4):
            ref[:, m * rows : (m + 1) * rows] = w[m // 2][(m % 2) * quart : (m % 2 + 1) * quart]

    def pair_up(ref, w):
        for m in range(2):
            ref[:, m * rows : (m + 1) * rows] = w[m].astype(BF16)

    def to_final(e):
        def body(k):
            if e not in QUARTER[k]:
                return
            a, b, both, _ = PAIRS[e]
            i = QUARTER[k].index(e)
            j = PARITY[k % 2].index(e)
            for kind in range(3):
                pltpu.make_async_copy(xr.at[i, kind], xr.at[i, kind], x_r.at[i, kind]).wait()
            parts = []
            for n in range(2):
                v = acc[e, band(r, n), :] + d2[j, band(r, n), :]
                for kind in range(3):
                    v += xr[i, kind, :, n * 2 * rows : (n + 1) * 2 * rows].astype(F32)
                parts.append(v * factor)
            bz = SLOTS[b][1]
            f = SENT[k].index(e) if e else None
            for n in range(2):
                w = [v[:, n * rows : (n + 1) * rows] for v in parts]
                if a == OWN:
                    fold(outb.at[(z + bz) % 4, n], w)
                else:
                    pair_up(fb.at[f, n], w)
                if both:
                    turned = jnp.concatenate(w, axis=0).T
                    pair_up(ftb.at[f, n], (turned[:short], turned[short:]))
            if e:
                for cp in final_copies(k, e):
                    cp.start()

        branches(body)

    for k in range(2):
        product(0, k)
    to_core(0)
    for slot in (Y1, Z1, Y3, Z3):
        for rr in (r, other):
            arrived(slot, rr, 0)
    to_x(0)
    early = (4, 6, 3, 5, 1, 2)
    for e in early:
        product(e, 0)
    for slot in (Y1, Z1, Y3, Z3):
        for rr in (r, other):
            arrived(slot, rr, 1)
    for n, rr in enumerate((r, other)):
        for slot in (Y1, Z1):
            forward(slot, rr, n, 0)
        for slot in (Y3, Z3):
            forward(slot, rr, n, 1)
    for n, e in enumerate(early):
        product(e, 1)
        to_core(e)
        if n:
            to_x(early[n - 1])
    to_x(early[-1])
    to_final(0)
    for e in early[:4]:
        to_final(e)
    for rr in (r, other):
        for k in range(2):
            arrived(Z2, rr, k)
        for k in range(2):
            product(7, k, rr)
    to_core(7)
    for k in range(2):
        for rr in (r, other):
            arrived(Y2, rr, k)
        product(8, k)
    to_core(8)
    to_x(7)
    for e in early[4:]:
        to_final(e)
    for k in range(2):
        product(9, k)
    to_core(9)
    to_x(8)
    to_x(9)
    for e in (7, 8, 9):
        to_final(e)

    local = ((0, 1), (0,), (), ())

    def finish(k):
        for dz in range(4):
            if dz in local[k]:
                continue
            for n in range(2):
                ref = got.at[(z + dz) % 4, n]
                pltpu.make_async_copy(ref, ref, f_r.at[(z + dz) % 4, n]).wait()
                v = ref[...].astype(F32)
                fold(outb.at[(z + dz) % 4, n], (v[:, 0:rows], v[:, rows : 2 * rows]))

    branches(finish)
    for i in range(8):
        for n in range(4):
            o_ref[n * quart : (n + 1) * quart, i * rows : (i + 1) * rows] = outb[
                i // 2, i % 2, :, n * rows : (n + 1) * rows
            ]

    for cp in done:
        cp.wait_send()

    def drain(k):
        for e in PARITY[1 - k % 2]:
            core_copy(k, e).wait_send()
        for e in PARITY[k % 2]:
            for i, kind in x_moves(k, e):
                x_copy(e, i, kind).wait_send()
        for e in QUARTER[k]:
            if e:
                for cp in final_copies(k, e):
                    cp.wait_send()

    branches(drain)


def gram(momentum):
    rows, cols = momentum.shape
    half = cols // 2
    n_rows = rows * lax.axis_size("tp")
    most = max(len(s) for s in QUARTER)
    sent = max(len(s) for s in SENT)
    dma = pltpu.SemaphoreType.DMA
    return pl.pallas_call(
        functools.partial(kernel, float(n_rows)),
        out_shape=jax.ShapeDtypeStruct((rows, 8 * rows), F32),
        in_specs=[pl.BlockSpec(memory_space=pl.ANY)],
        out_specs=pl.BlockSpec(memory_space=pltpu.VMEM),
        scratch_shapes=[
            pltpu.VMEM((len(SLOTS), 2 * rows, half), BF16),
            pltpu.VMEM((rows, half), BF16),
            pltpu.VMEM((len(PAIRS), 2 * rows, 2 * rows), F32),
            pltpu.VMEM((5, 2 * rows, 2 * rows), F32),
            pltpu.VMEM((most, 3, rows // 2, 4 * rows), BF16),
            pltpu.VMEM((most, 3, rows // 2, 4 * rows), BF16),
            pltpu.VMEM((sent, 2, rows // 2, 2 * rows), BF16),
            pltpu.VMEM((sent, 2, rows // 2, 2 * rows), BF16),
            pltpu.VMEM((4, 2, rows // 2, 2 * rows), BF16),
            pltpu.VMEM((4, 2, rows // 4, 4 * rows), F32),
            pltpu.VMEM((3, 8, 128), F32),
            pltpu.VMEM((8, 8, 128), F32),
            pltpu.VMEM((4, 8, 128), F32),
            pltpu.VMEM((4, 8, 128), F32),
            dma((cols // CHUNK,)),
            dma((24,)),
            dma((3, 8)),
            dma((4, 2, 2)),
            dma((len(SLOTS), 2, 2)),
            dma((2, 2, 2)),
            dma((2,)),
            dma((5,)),
            dma((5,)),
            dma((most, 3)),
            dma((most, 3)),
            dma((sent, 4)),
            dma((4, 2)),
        ],
        compiler_params=pltpu.CompilerParams(
            collective_id=0, has_side_effects=True, vmem_limit_bytes=62 * 2**20
        ),
        cost_estimate=pl.CostEstimate(
            flops=2 * 10 * (2 * rows) ** 2 * half, bytes_accessed=4 * rows * (cols + 8 * rows), transcendentals=0
        ),
    )(momentum)


def solution(mesh):
    return jax.shard_map(gram, mesh=mesh, in_specs=(P("tp", "col"),), out_specs=P("tp", "col"), check_vma=False)
```

```python
import functools

import jax
import jax.numpy as jnp
from jax import lax
from jax.experimental import pallas as pl
from jax.experimental.pallas import tpu as pltpu
from jax.sharding import PartitionSpec as P

SLOTS = ((0, 0), (1, 0), (3, 0), (0, 1), (0, 3), (2, 0), (0, 2))
OWN, Y1, Y3, Z1, Z3, Y2, Z2 = range(7)
PAIRS = (
    (OWN, OWN, False, 0),
    (OWN, Z1, True, 0),
    (Z3, Z1, False, 2),
    (OWN, Y1, True, 1),
    (Z1, Y1, True, 1),
    (Y1, Y3, False, 3),
    (Z1, Y3, True, 3),
    (Z2, Y3, True, 3),
    (Z1, Y2, True, 2),
    (Y2, Z2, False, 0),
)
QUARTER = tuple(tuple(e for e, p in enumerate(PAIRS) if p[3] == q) for q in range(4))
PARITY = tuple(tuple(sorted(QUARTER[p] + QUARTER[p + 2])) for p in range(2))
SENT = tuple(tuple(e for e in q if e) for q in QUARTER)
MESH = pl.DeviceIdType.MESH
F32, BF16 = jnp.float32, jnp.bfloat16
CHUNK = 384


def kernel(
    factor, m_ref, o_ref,
    slots, xsend, acc, d2, xs, xr, fb, ftb, got, outb, part, g8, gy, gz,
    in_sem, ps_s, ps_r, gat_s, gat_r, fwd_s, xc_s, d2_s, d2_r, x_s, x_r, f_s, f_r,
):
    rows = m_ref.shape[0]
    half = m_ref.shape[1] // 2
    cut = (half // 2) // 256 * 256
    spans = ((0, cut), (cut, half - cut))
    t, c = lax.axis_index("tp"), lax.axis_index("col")
    y, z, r = t // 8, (t // 2) % 4, t % 2
    q = (c - y + 4) % 4
    per_half = half // CHUNK

    def at(dy=0, dz=0, xl=None, dc=0):
        xl = r if xl is None else xl
        return ((((y + dy) % 4) * 4 + (z + dz) % 4) * 2 + xl, (c + dc + 4) % 4)

    core_peer = (t, c + 1 - 2 * (c % 2))
    other = 1 - r

    loads = []
    for j in range(2 * per_half):
        dst = acc.at[j // 2, pl.ds((j % 2) * rows, rows), pl.ds(0, CHUNK)]
        loads.append(pltpu.make_async_copy(m_ref.at[:, pl.ds(j * CHUNK, CHUNK)], dst, in_sem.at[j]))
        loads[-1].start()

    bar = pltpu.get_barrier_semaphore()
    me8 = r * 4 + c

    def at8(i):
        return ((y * 4 + z) * 2 + i // 4, i % 4)

    greet = [at8((me8 + o) % 8) for o in range(1, 8)]
    greet += [at(dy=o) for o in range(1, 4)] + [at(dz=o) for o in range(1, 4)]
    greet += [at(dz=1, xl=other), at(dz=3, xl=other), at(dz=1, dc=2), at(dz=3, dc=2)]
    for dy, dc in ((1, 3), (3, 1), (2, 2)):
        greet += [at(dy=dy, xl=r, dc=dc), at(dy=dy, xl=other, dc=dc)]
    for dev in greet:
        pl.semaphore_signal(bar, inc=1, device_id=dev, device_id_type=MESH)

    total = jnp.zeros((8, CHUNK), F32)
    for j in range(2 * per_half):
        loads[j].wait()
        v = acc[j // 2, (j % 2) * rows : (j % 2 + 1) * rows, 0:CHUNK]
        total += jnp.sum((v * v).reshape(rows // 8, 8, CHUNK), axis=0)
    part[0] = total[:, 0:128] + total[:, 128:256] + total[:, 256:384]
    pl.semaphore_wait(bar, len(greet))
    done = []

    def share(stage, place, me, n, device):
        place[pl.ds(me, 1)] = part[stage][None]
        copies = []
        for o in range(1, n):
            i = 8 * stage + o
            copies.append(
                pltpu.make_async_remote_copy(
                    part.at[stage], place.at[me], ps_s.at[i], ps_r.at[stage, o],
                    device_id=device(o), device_id_type=MESH,
                )
            )
            copies[-1].start()
        for o in range(1, n):
            copies[o - 1].wait_recv()
        done.extend(copies)
        return jnp.sum(place[...], axis=0)

    part[1] = share(0, g8, me8, 8, lambda o: at8((me8 + o) % 8))
    part[2] = share(1, gy, y, 4, lambda o: at(dy=o))
    whole = share(2, gz, z, 4, lambda o: at(dz=o))
    total = jnp.sum(jnp.sum(whole, axis=0, keepdims=True), axis=1, keepdims=True)
    scale = 1.0 / (jnp.sqrt(total) + 1e-07)

    def normalize(which, n0, n1, store):
        for n in range(n0, n1):
            v = acc[which * (per_half // 2) + n // 2, (n % 2) * rows : (n % 2 + 1) * rows, 0:CHUNK]
            store(n, (v * scale).astype(BF16))

    mine = pl.ds(pl.multiple_of(r * rows, 16), rows)
    theirs = pl.ds(pl.multiple_of(other * rows, 16), rows)

    def to_own(n, v):
        slots[OWN, mine, n * CHUNK : (n + 1) * CHUNK] = v

    def to_send(n, v):
        xsend[:, n * CHUNK : (n + 1) * CHUNK] = v

    def unit(slot, rr, k):
        start = pl.ds(pl.multiple_of(rr * rows, 16), rows)
        return slots.at[slot, start, pl.ds(*spans[k])]

    direct = ((Y1, at(dy=3)), (Y3, at(dy=1)), (Z1, at(dz=3)), (Z3, at(dz=1)))

    def send_own(rr, second, k):
        for i, (slot, dev) in enumerate(direct):
            cp = pltpu.make_async_remote_copy(
                unit(OWN, rr, k), unit(slot, rr, k), gat_s.at[i, second, k], gat_r.at[slot, rr, k],
                device_id=dev, device_id_type=MESH,
            )
            cp.start()
            done.append(cp)

    def arrived(slot, rr, k):
        ref = unit(slot, rr, k)
        pltpu.make_async_copy(ref, ref, gat_r.at[slot, rr, k]).wait()

    def send_x(k):
        cp = pltpu.make_async_remote_copy(
            xsend.at[:, pl.ds(*spans[k])], unit(OWN, r, k), xc_s.at[k], gat_r.at[OWN, r, k],
            device_id=at(xl=other), device_id_type=MESH,
        )
        cp.start()
        done.append(cp)

    onward = {Y1: (0, Y2, at(dy=3)), Z1: (1, Z2, at(dz=3)), Y3: (0, Y2, at(dy=1)), Z3: (1, Z2, at(dz=1))}

    def forward(slot, rr, second, k):
        i, to, dev = onward[slot]
        cp = pltpu.make_async_remote_copy(
            unit(slot, rr, k), unit(to, rr, k), fwd_s.at[i, second, k], gat_r.at[to, rr, k],
            device_id=dev, device_id_type=MESH,
        )
        cp.start()
        done.append(cp)

    first_cut = -(-cut // CHUNK)
    normalize(r, 0, first_cut, to_own)
    send_own(r, 0, 0)
    normalize(other, 0, first_cut, to_send)
    send_x(0)
    normalize(other, first_cut, per_half, to_send)
    normalize(r, first_cut, per_half, to_own)

    tile = 192

    def product(e, k, rr=None):
        a, b = PAIRS[e][:2]
        cols = pl.ds(*spans[k])
        size = tile if rr is None else tile // 2
        base = 0 if rr is None else rr * rows
        n = 2 * rows // tile

        def step(i, _):
            here = pl.ds(pl.multiple_of(base + i * size, size), size)
            p = lax.dot_general(
                slots[a, here, cols], slots[b, :, cols], (((1,), (1,)), ((), ())), preferred_element_type=F32
            )
            if k == 0:
                acc[e, here, :] = p
            else:
                acc[e, here, :] += p
            return 0

        lax.fori_loop(0, n, step, 0)

    arrived(OWN, other, 0)
    send_x(1)
    send_own(other, 1, 0)
    send_own(r, 0, 1)
    arrived(OWN, other, 1)
    send_own(other, 1, 1)

    def branches(body):
        for k in range(4):
            @pl.when(q == k)
            def _(k=k):
                body(k)

    def core_copy(k, e):
        i = PARITY[1 - k % 2].index(e)
        return pltpu.make_async_remote_copy(
            acc.at[e], d2.at[i], d2_s.at[i], d2_r.at[i], device_id=core_peer, device_id_type=MESH
        )

    def to_core(e):
        def body(k):
            if e in PARITY[1 - k % 2]:
                core_copy(k, e).start()

        branches(body)

    def x_copy(e, i, kind):
        dev = (at(xl=other), at(dc=2), at(xl=other, dc=2))[kind]
        return pltpu.make_async_remote_copy(
            xs.at[i, kind], xr.at[i, kind], x_s.at[i, kind], x_r.at[i, kind], device_id=dev, device_id_type=MESH
        )

    def x_moves(k, e):
        if e in QUARTER[k]:
            return [(QUARTER[k].index(e), 0)]
        i = QUARTER[(k + 2) % 4].index(e)
        return [(i, 1), (i, 2)]

    short = rows // 2

    def band(rr, n):
        return pl.ds(pl.multiple_of(rr * rows + n * short, 16), short)

    def to_x(e):
        def body(k):
            if e not in PARITY[k % 2]:
                return
            j = PARITY[k % 2].index(e)
            pltpu.make_async_copy(d2.at[j], d2.at[j], d2_r.at[j]).wait()
            for i, kind in x_moves(k, e):
                rr = r if kind == 1 else other
                for n in range(2):
                    v = acc[e, band(rr, n), :] + d2[j, band(rr, n), :]
                    xs[i, kind, :, n * 2 * rows : (n + 1) * 2 * rows] = v.astype(BF16)
                x_copy(e, i, kind).start()

        branches(body)

    def final_copies(k, e):
        a, b, both, q_e = PAIRS[e]
        i = SENT[k].index(e)
        (ay, az), (by, bz) = SLOTS[a], SLOTS[b]
        copies = []
        if a != OWN:
            for n in range(2):
                copies.append(
                    pltpu.make_async_remote_copy(
                        fb.at[i, n], got.at[(z + bz) % 4, n], f_s.at[i, n], f_r.at[(z + bz) % 4, n],
                        device_id=at(ay, az, dc=by - q_e), device_id_type=MESH,
                    )
                )
        if both:
            for n in range(2):
                copies.append(
                    pltpu.make_async_remote_copy(
                        ftb.at[i, n], got.at[(z + az) % 4, r], f_s.at[i, 2 + n], f_r.at[(z + az) % 4, r],
                        device_id=at(by, bz, xl=n, dc=ay - q_e), device_id_type=MESH,
                    )
                )
        return copies

    quart = rows // 4

    def fold(ref, w):
        for m in range(4):
            ref[:, m * rows : (m + 1) * rows] = w[m // 2][(m % 2) * quart : (m % 2 + 1) * quart]

    def pair_up(ref, w):
        for m in range(2):
            ref[:, m * rows : (m + 1) * rows] = w[m].astype(BF16)

    def to_final(e):
        def body(k):
            if e not in QUARTER[k]:
                return
            a, b, both, _ = PAIRS[e]
            i = QUARTER[k].index(e)
            j = PARITY[k % 2].index(e)
            for kind in range(3):
                pltpu.make_async_copy(xr.at[i, kind], xr.at[i, kind], x_r.at[i, kind]).wait()
            parts = []
            for n in range(2):
                v = acc[e, band(r, n), :] + d2[j, band(r, n), :]
                for kind in range(3):
                    v += xr[i, kind, :, n * 2 * rows : (n + 1) * 2 * rows].astype(F32)
                parts.append(v * factor)
            bz = SLOTS[b][1]
            f = SENT[k].index(e) if e else None
            for n in range(2):
                w = [v[:, n * rows : (n + 1) * rows] for v in parts]
                if a == OWN:
                    fold(outb.at[(z + bz) % 4, n], w)
                else:
                    pair_up(fb.at[f, n], w)
                if both:
                    turned = jnp.concatenate(w, axis=0).T
                    pair_up(ftb.at[f, n], (turned[:short], turned[short:]))
            if e:
                for cp in final_copies(k, e):
                    cp.start()

        branches(body)

    for k in range(2):
        product(0, k)
    to_core(0)
    for slot in (Y1, Z1, Y3, Z3):
        for rr in (r, other):
            arrived(slot, rr, 0)
    to_x(0)
    early = (2, 6, 4, 5, 3, 1)
    for e in early:
        product(e, 0)
    for slot in (Y1, Z1, Y3, Z3):
        for rr in (r, other):
            arrived(slot, rr, 1)
    for n, rr in enumerate((r, other)):
        for slot in (Y1, Z1):
            forward(slot, rr, n, 0)
        for slot in (Y3, Z3):
            forward(slot, rr, n, 1)
    for n, e in enumerate(early):
        product(e, 1)
        to_core(e)
        if n:
            to_x(early[n - 1])
    to_x(early[-1])
    to_final(0)
    for e in early[:4]:
        to_final(e)
    for rr in (r, other):
        for k in range(2):
            arrived(Z2, rr, k)
        for k in range(2):
            product(7, k, rr)
    to_core(7)
    for k in range(2):
        for rr in (r, other):
            arrived(Y2, rr, k)
        product(8, k)
    to_core(8)
    to_x(7)
    for e in early[4:]:
        to_final(e)
    for k in range(2):
        product(9, k)
    to_core(9)
    to_x(8)
    to_x(9)
    for e in (7, 8, 9):
        to_final(e)

    local = ((0, 1), (0,), (), ())

    def finish(k):
        for dz in range(4):
            if dz in local[k]:
                continue
            for n in range(2):
                ref = got.at[(z + dz) % 4, n]
                pltpu.make_async_copy(ref, ref, f_r.at[(z + dz) % 4, n]).wait()
                v = ref[...].astype(F32)
                fold(outb.at[(z + dz) % 4, n], (v[:, 0:rows], v[:, rows : 2 * rows]))

    branches(finish)
    for i in range(8):
        for n in range(4):
            o_ref[n * quart : (n + 1) * quart, i * rows : (i + 1) * rows] = outb[
                i // 2, i % 2, :, n * rows : (n + 1) * rows
            ]

    for cp in done:
        cp.wait_send()

    def drain(k):
        for e in PARITY[1 - k % 2]:
            core_copy(k, e).wait_send()
        for e in PARITY[k % 2]:
            for i, kind in x_moves(k, e):
                x_copy(e, i, kind).wait_send()
        for e in QUARTER[k]:
            if e:
                for cp in final_copies(k, e):
                    cp.wait_send()

    branches(drain)


def gram(momentum):
    rows, cols = momentum.shape
    half = cols // 2
    n_rows = rows * lax.axis_size("tp")
    most = max(len(s) for s in QUARTER)
    sent = max(len(s) for s in SENT)
    dma = pltpu.SemaphoreType.DMA
    return pl.pallas_call(
        functools.partial(kernel, float(n_rows)),
        out_shape=jax.ShapeDtypeStruct((rows, 8 * rows), F32),
        in_specs=[pl.BlockSpec(memory_space=pl.ANY)],
        out_specs=pl.BlockSpec(memory_space=pltpu.VMEM),
        scratch_shapes=[
            pltpu.VMEM((len(SLOTS), 2 * rows, half), BF16),
            pltpu.VMEM((rows, half), BF16),
            pltpu.VMEM((len(PAIRS), 2 * rows, 2 * rows), F32),
            pltpu.VMEM((5, 2 * rows, 2 * rows), F32),
            pltpu.VMEM((most, 3, rows // 2, 4 * rows), BF16),
            pltpu.VMEM((most, 3, rows // 2, 4 * rows), BF16),
            pltpu.VMEM((sent, 2, rows // 2, 2 * rows), BF16),
            pltpu.VMEM((sent, 2, rows // 2, 2 * rows), BF16),
            pltpu.VMEM((4, 2, rows // 2, 2 * rows), BF16),
            pltpu.VMEM((4, 2, rows // 4, 4 * rows), F32),
            pltpu.VMEM((3, 8, 128), F32),
            pltpu.VMEM((8, 8, 128), F32),
            pltpu.VMEM((4, 8, 128), F32),
            pltpu.VMEM((4, 8, 128), F32),
            dma((cols // CHUNK,)),
            dma((24,)),
            dma((3, 8)),
            dma((4, 2, 2)),
            dma((len(SLOTS), 2, 2)),
            dma((2, 2, 2)),
            dma((2,)),
            dma((5,)),
            dma((5,)),
            dma((most, 3)),
            dma((most, 3)),
            dma((sent, 4)),
            dma((4, 2)),
        ],
        compiler_params=pltpu.CompilerParams(
            collective_id=0, has_side_effects=True, vmem_limit_bytes=62 * 2**20
        ),
        cost_estimate=pl.CostEstimate(
            flops=2 * 10 * (2 * rows) ** 2 * half, bytes_accessed=4 * rows * (cols + 8 * rows), transcendentals=0
        ),
    )(momentum)


def solution(mesh):
    return jax.shard_map(gram, mesh=mesh, in_specs=(P("tp", "col"),), out_specs=P("tp", "col"), check_vma=False)
```

```python
import functools

import jax
import jax.numpy as jnp
from jax import lax
from jax.experimental import pallas as pl
from jax.experimental.pallas import tpu as pltpu
from jax.sharding import PartitionSpec as P

SLOTS = ((0, 0), (1, 0), (3, 0), (0, 1), (0, 3), (2, 0), (0, 2))
OWN, Y1, Y3, Z1, Z3, Y2, Z2 = range(7)
PAIRS = (
    (OWN, OWN, False, 0),
    (OWN, Z1, True, 0),
    (Z3, Z1, False, 2),
    (OWN, Y1, True, 1),
    (Z1, Y1, True, 1),
    (Y1, Y3, False, 3),
    (Z1, Y3, True, 3),
    (Z2, Y3, True, 3),
    (Z1, Y2, True, 2),
    (Y2, Z2, False, 0),
)
QUARTER = tuple(tuple(e for e, p in enumerate(PAIRS) if p[3] == q) for q in range(4))
PARITY = tuple(tuple(sorted(QUARTER[p] + QUARTER[p + 2])) for p in range(2))
SENT = tuple(tuple(e for e in q if e) for q in QUARTER)
MESH = pl.DeviceIdType.MESH
F32, BF16 = jnp.float32, jnp.bfloat16
CHUNK = 384


def kernel(
    factor, m_ref, o_ref,
    slots, xsend, acc, d2, xs, xr, fb, ftb, got, outb, part, g8, gy, gz,
    in_sem, ps_s, ps_r, gat_s, gat_r, fwd_s, xc_s, d2_s, d2_r, x_s, x_r, f_s, f_r,
):
    rows = m_ref.shape[0]
    half = m_ref.shape[1] // 2
    cut = (half // 2) // 256 * 256
    spans = ((0, cut), (cut, half - cut))
    t, c = lax.axis_index("tp"), lax.axis_index("col")
    y, z, r = t // 8, (t // 2) % 4, t % 2
    q = (c - y + 4) % 4
    per_half = half // CHUNK

    def at(dy=0, dz=0, xl=None, dc=0):
        xl = r if xl is None else xl
        return ((((y + dy) % 4) * 4 + (z + dz) % 4) * 2 + xl, (c + dc + 4) % 4)

    core_peer = (t, c + 1 - 2 * (c % 2))
    other = 1 - r

    loads = []
    for j in range(2 * per_half):
        dst = acc.at[j // 2, pl.ds((j % 2) * rows, rows), pl.ds(0, CHUNK)]
        loads.append(pltpu.make_async_copy(m_ref.at[:, pl.ds(j * CHUNK, CHUNK)], dst, in_sem.at[j]))
        loads[-1].start()

    bar = pltpu.get_barrier_semaphore()
    me8 = r * 4 + c

    def at8(i):
        return ((y * 4 + z) * 2 + i // 4, i % 4)

    greet = [at8((me8 + o) % 8) for o in range(1, 8)]
    greet += [at(dy=o) for o in range(1, 4)] + [at(dz=o) for o in range(1, 4)]
    greet += [at(dz=1, xl=other), at(dz=3, xl=other), at(dz=1, dc=2), at(dz=3, dc=2)]
    for dy, dc in ((1, 3), (3, 1), (2, 2)):
        greet += [at(dy=dy, xl=r, dc=dc), at(dy=dy, xl=other, dc=dc)]
    for dev in greet:
        pl.semaphore_signal(bar, inc=1, device_id=dev, device_id_type=MESH)

    total = jnp.zeros((8, CHUNK), F32)
    for j in range(2 * per_half):
        loads[j].wait()
        v = acc[j // 2, (j % 2) * rows : (j % 2 + 1) * rows, 0:CHUNK]
        total += jnp.sum((v * v).reshape(rows // 8, 8, CHUNK), axis=0)
    part[0] = total[:, 0:128] + total[:, 128:256] + total[:, 256:384]
    pl.semaphore_wait(bar, len(greet))
    done = []

    def share(stage, place, me, n, device):
        place[pl.ds(me, 1)] = part[stage][None]
        copies = []
        for o in range(1, n):
            i = 8 * stage + o
            copies.append(
                pltpu.make_async_remote_copy(
                    part.at[stage], place.at[me], ps_s.at[i], ps_r.at[stage, o],
                    device_id=device(o), device_id_type=MESH,
                )
            )
            copies[-1].start()
        for o in range(1, n):
            copies[o - 1].wait_recv()
        done.extend(copies)
        return jnp.sum(place[...], axis=0)

    part[1] = share(0, g8, me8, 8, lambda o: at8((me8 + o) % 8))
    part[2] = share(1, gy, y, 4, lambda o: at(dy=o))
    whole = share(2, gz, z, 4, lambda o: at(dz=o))
    total = jnp.sum(jnp.sum(whole, axis=0, keepdims=True), axis=1, keepdims=True)
    scale = 1.0 / (jnp.sqrt(total) + 1e-07)

    def normalize(which, n0, n1, store):
        for n in range(n0, n1):
            v = acc[which * (per_half // 2) + n // 2, (n % 2) * rows : (n % 2 + 1) * rows, 0:CHUNK]
            store(n, (v * scale).astype(BF16))

    mine = pl.ds(pl.multiple_of(r * rows, 16), rows)
    theirs = pl.ds(pl.multiple_of(other * rows, 16), rows)

    def to_own(n, v):
        slots[OWN, mine, n * CHUNK : (n + 1) * CHUNK] = v

    def to_send(n, v):
        xsend[:, n * CHUNK : (n + 1) * CHUNK] = v

    def unit(slot, rr, k):
        start = pl.ds(pl.multiple_of(rr * rows, 16), rows)
        return slots.at[slot, start, pl.ds(*spans[k])]

    direct = ((Y1, at(dy=3)), (Y3, at(dy=1)), (Z1, at(dz=3)), (Z3, at(dz=1)))

    def send_own(rr, second, k):
        for i, (slot, dev) in enumerate(direct):
            cp = pltpu.make_async_remote_copy(
                unit(OWN, rr, k), unit(slot, rr, k), gat_s.at[i, second, k], gat_r.at[slot, rr, k],
                device_id=dev, device_id_type=MESH,
            )
            cp.start()
            done.append(cp)

    def arrived(slot, rr, k):
        ref = unit(slot, rr, k)
        pltpu.make_async_copy(ref, ref, gat_r.at[slot, rr, k]).wait()

    def send_x(k):
        cp = pltpu.make_async_remote_copy(
            xsend.at[:, pl.ds(*spans[k])], unit(OWN, r, k), xc_s.at[k], gat_r.at[OWN, r, k],
            device_id=at(xl=other), device_id_type=MESH,
        )
        cp.start()
        done.append(cp)

    onward = {Y1: (0, Y2, at(dy=3)), Z1: (1, Z2, at(dz=3)), Y3: (0, Y2, at(dy=1)), Z3: (1, Z2, at(dz=1))}

    def forward(slot, rr, second, k):
        i, to, dev = onward[slot]
        cp = pltpu.make_async_remote_copy(
            unit(slot, rr, k), unit(to, rr, k), fwd_s.at[i, second, k], gat_r.at[to, rr, k],
            device_id=dev, device_id_type=MESH,
        )
        cp.start()
        done.append(cp)

    first_cut = -(-cut // CHUNK)
    normalize(r, 0, first_cut, to_own)
    send_own(r, 0, 0)
    normalize(other, 0, first_cut, to_send)
    send_x(0)
    normalize(other, first_cut, per_half, to_send)
    normalize(r, first_cut, per_half, to_own)

    tile = 192

    def product(e, k, rr=None):
        a, b = PAIRS[e][:2]
        cols = pl.ds(*spans[k])
        size = tile if rr is None else tile // 2
        base = 0 if rr is None else rr * rows
        n = 2 * rows // tile

        def step(i, _):
            here = pl.ds(pl.multiple_of(base + i * size, size), size)
            p = lax.dot_general(
                slots[a, here, cols], slots[b, :, cols], (((1,), (1,)), ((), ())), preferred_element_type=F32
            )
            if k == 0:
                acc[e, here, :] = p
            else:
                acc[e, here, :] += p
            return 0

        lax.fori_loop(0, n, step, 0)

    arrived(OWN, other, 0)
    send_x(1)
    send_own(other, 1, 0)
    send_own(r, 0, 1)
    arrived(OWN, other, 1)
    send_own(other, 1, 1)

    def branches(body):
        for k in range(4):
            @pl.when(q == k)
            def _(k=k):
                body(k)

    def core_copy(k, e):
        i = PARITY[1 - k % 2].index(e)
        return pltpu.make_async_remote_copy(
            acc.at[e], d2.at[i], d2_s.at[i], d2_r.at[i], device_id=core_peer, device_id_type=MESH
        )

    def to_core(e):
        def body(k):
            if e in PARITY[1 - k % 2]:
                core_copy(k, e).start()

        branches(body)

    def x_copy(e, i, kind):
        dev = (at(xl=other), at(dc=2), at(xl=other, dc=2))[kind]
        return pltpu.make_async_remote_copy(
            xs.at[i, kind], xr.at[i, kind], x_s.at[i, kind], x_r.at[i, kind], device_id=dev, device_id_type=MESH
        )

    def x_moves(k, e):
        if e in QUARTER[k]:
            return [(QUARTER[k].index(e), 0)]
        i = QUARTER[(k + 2) % 4].index(e)
        return [(i, 1), (i, 2)]

    short = rows // 2

    def band(rr, n):
        return pl.ds(pl.multiple_of(rr * rows + n * short, 16), short)

    def to_x(e):
        def body(k):
            if e not in PARITY[k % 2]:
                return
            j = PARITY[k % 2].index(e)
            pltpu.make_async_copy(d2.at[j], d2.at[j], d2_r.at[j]).wait()
            for i, kind in x_moves(k, e):
                rr = r if kind == 1 else other
                for n in range(2):
                    v = acc[e, band(rr, n), :] + d2[j, band(rr, n), :]
                    xs[i, kind, :, n * 2 * rows : (n + 1) * 2 * rows] = v.astype(BF16)
                x_copy(e, i, kind).start()

        branches(body)

    def final_copies(k, e):
        a, b, both, q_e = PAIRS[e]
        i = SENT[k].index(e)
        (ay, az), (by, bz) = SLOTS[a], SLOTS[b]
        copies = []
        if a != OWN:
            for n in range(2):
                copies.append(
                    pltpu.make_async_remote_copy(
                        fb.at[i, n], got.at[(z + bz) % 4, n], f_s.at[i, n], f_r.at[(z + bz) % 4, n],
                        device_id=at(ay, az, dc=by - q_e), device_id_type=MESH,
                    )
                )
        if both:
            for n in range(2):
                copies.append(
                    pltpu.make_async_remote_copy(
                        ftb.at[i, n], got.at[(z + az) % 4, r], f_s.at[i, 2 + n], f_r.at[(z + az) % 4, r],
                        device_id=at(by, bz, xl=n, dc=ay - q_e), device_id_type=MESH,
                    )
                )
        return copies

    quart = rows // 4

    def fold(ref, w):
        for m in range(4):
            ref[:, m * rows : (m + 1) * rows] = w[m // 2][(m % 2) * quart : (m % 2 + 1) * quart]

    def pair_up(ref, w):
        for m in range(2):
            ref[:, m * rows : (m + 1) * rows] = w[m].astype(BF16)

    def to_final(e):
        def body(k):
            if e not in QUARTER[k]:
                return
            a, b, both, _ = PAIRS[e]
            i = QUARTER[k].index(e)
            j = PARITY[k % 2].index(e)
            for kind in range(3):
                pltpu.make_async_copy(xr.at[i, kind], xr.at[i, kind], x_r.at[i, kind]).wait()
            parts = []
            for n in range(2):
                v = acc[e, band(r, n), :] + d2[j, band(r, n), :]
                for kind in range(3):
                    v += xr[i, kind, :, n * 2 * rows : (n + 1) * 2 * rows].astype(F32)
                parts.append(v * factor)
            bz = SLOTS[b][1]
            f = SENT[k].index(e) if e else None
            for n in range(2):
                w = [v[:, n * rows : (n + 1) * rows] for v in parts]
                if a == OWN:
                    fold(outb.at[(z + bz) % 4, n], w)
                else:
                    pair_up(fb.at[f, n], w)
                if both:
                    turned = jnp.concatenate(w, axis=0).T
                    pair_up(ftb.at[f, n], (turned[:short], turned[short:]))
            if e:
                for cp in final_copies(k, e):
                    cp.start()

        branches(body)

    for k in range(2):
        product(0, k)
    to_core(0)
    for slot in (Y1, Z1, Y3, Z3):
        for rr in (r, other):
            arrived(slot, rr, 0)
    to_x(0)
    early = (2, 6, 4, 5, 3, 1)
    for e in early:
        product(e, 0)
    for slot in (Y1, Z1, Y3, Z3):
        for rr in (r, other):
            arrived(slot, rr, 1)
    for n, rr in enumerate((r, other)):
        for slot in (Y1, Z1):
            forward(slot, rr, n, 0)
        for slot in (Y3, Z3):
            forward(slot, rr, n, 1)
    for n, e in enumerate(early):
        product(e, 1)
        to_core(e)
        if n:
            to_x(early[n - 1])
    to_x(early[-1])
    to_final(0)
    for e in early[:4]:
        to_final(e)
    for rr in (r, other):
        for k in range(2):
            arrived(Z2, rr, k)
        for k in range(2):
            product(7, k, rr)
    to_core(7)
    for k in range(2):
        for rr in (r, other):
            arrived(Y2, rr, k)
        product(8, k)
    to_core(8)
    to_x(7)
    for k in range(2):
        product(9, k)
    to_core(9)
    to_x(8)
    for e in early[4:]:
        to_final(e)
    to_x(9)
    for e in (7, 8, 9):
        to_final(e)

    local = ((0, 1), (0,), (), ())

    def finish(k):
        for dz in range(4):
            if dz in local[k]:
                continue
            for n in range(2):
                ref = got.at[(z + dz) % 4, n]
                pltpu.make_async_copy(ref, ref, f_r.at[(z + dz) % 4, n]).wait()
                v = ref[...].astype(F32)
                fold(outb.at[(z + dz) % 4, n], (v[:, 0:rows], v[:, rows : 2 * rows]))

    branches(finish)
    for i in range(8):
        for n in range(4):
            o_ref[n * quart : (n + 1) * quart, i * rows : (i + 1) * rows] = outb[
                i // 2, i % 2, :, n * rows : (n + 1) * rows
            ]

    for cp in done:
        cp.wait_send()

    def drain(k):
        for e in PARITY[1 - k % 2]:
            core_copy(k, e).wait_send()
        for e in PARITY[k % 2]:
            for i, kind in x_moves(k, e):
                x_copy(e, i, kind).wait_send()
        for e in QUARTER[k]:
            if e:
                for cp in final_copies(k, e):
                    cp.wait_send()

    branches(drain)


def gram(momentum):
    rows, cols = momentum.shape
    half = cols // 2
    n_rows = rows * lax.axis_size("tp")
    most = max(len(s) for s in QUARTER)
    sent = max(len(s) for s in SENT)
    dma = pltpu.SemaphoreType.DMA
    return pl.pallas_call(
        functools.partial(kernel, float(n_rows)),
        out_shape=jax.ShapeDtypeStruct((rows, 8 * rows), F32),
        in_specs=[pl.BlockSpec(memory_space=pl.ANY)],
        out_specs=pl.BlockSpec(memory_space=pltpu.VMEM),
        scratch_shapes=[
            pltpu.VMEM((len(SLOTS), 2 * rows, half), BF16),
            pltpu.VMEM((rows, half), BF16),
            pltpu.VMEM((len(PAIRS), 2 * rows, 2 * rows), F32),
            pltpu.VMEM((5, 2 * rows, 2 * rows), F32),
            pltpu.VMEM((most, 3, rows // 2, 4 * rows), BF16),
            pltpu.VMEM((most, 3, rows // 2, 4 * rows), BF16),
            pltpu.VMEM((sent, 2, rows // 2, 2 * rows), BF16),
            pltpu.VMEM((sent, 2, rows // 2, 2 * rows), BF16),
            pltpu.VMEM((4, 2, rows // 2, 2 * rows), BF16),
            pltpu.VMEM((4, 2, rows // 4, 4 * rows), F32),
            pltpu.VMEM((3, 8, 128), F32),
            pltpu.VMEM((8, 8, 128), F32),
            pltpu.VMEM((4, 8, 128), F32),
            pltpu.VMEM((4, 8, 128), F32),
            dma((cols // CHUNK,)),
            dma((24,)),
            dma((3, 8)),
            dma((4, 2, 2)),
            dma((len(SLOTS), 2, 2)),
            dma((2, 2, 2)),
            dma((2,)),
            dma((5,)),
            dma((5,)),
            dma((most, 3)),
            dma((most, 3)),
            dma((sent, 4)),
            dma((4, 2)),
        ],
        compiler_params=pltpu.CompilerParams(
            collective_id=0, has_side_effects=True, vmem_limit_bytes=62 * 2**20
        ),
        cost_estimate=pl.CostEstimate(
            flops=2 * 10 * (2 * rows) ** 2 * half, bytes_accessed=4 * rows * (cols + 8 * rows), transcendentals=0
        ),
    )(momentum)


def solution(mesh):
    return jax.shard_map(gram, mesh=mesh, in_specs=(P("tp", "col"),), out_specs=P("tp", "col"), check_vma=False)
```
